32 devices in a mesh: rep: 4 (over y, x), blk: 8 (over z, core).
Axes of the slice: x: 2, y: 2, z: 4, core: 2. Of those that a mesh axis runs over, the one named last changes fastest.
Arguments:
- features: bfloat16 [16384, 128], P(('rep', 'blk')), may hold values from -6 to 6
- degrees: int32 [16384], P(('rep', 'blk')), may hold values from 1 to 32
- tile_weights: bfloat16 [4, 8, 160, 128, 128], P('rep', 'blk'), may hold values from 0 to 0.049804688
- tile_rows: int32 [4, 8, 160], P('rep', 'blk'), may hold values from 0 to 31, as said below
- tile_cols: int32 [4, 8, 160], P('rep', 'blk'), may hold values from 0 to 15, as said below
- tile_counts: int32 [4, 8], P('rep', 'blk'), may hold values from 1 to 160, as said below
- weight: bfloat16 [128, 256], replicated, may hold values from -0.5 to 0.5
- layer_bias: float32 [256], replicated, may hold values from -3 to 3
- upstream: bfloat16 [16384, 256], P(('rep', 'blk')), may hold values from -6 to 6
Outputs:
- hidden: bfloat16 [16384, 256], P(('rep', 'blk'))
- feature_grad: bfloat16 [16384, 128], P(('rep', 'blk'))
- weight_grad: float32 [128, 256], replicated
- bias_grad: float32 [256], replicated
The draws below stay inside these ranges and needn't reach their ends.
Inputs may be any that keep to these rules, and one draw needn't show every extreme that they name: `tile_rows`: the first tile_counts slots of a device hold distinct tiles, ordered by row and then by column; a used row h lies in node block r * 8 + h // 4, whose index h // 4 is within 3 steps of the device's blk index around the loop of 8; unused slots hold the device's own first tile row. `tile_cols`: unused slots hold 0. `tile_counts`: at most 40 used slots of one device lie in the rows of one node block; this and the largest count are both reached by some device in every draw.
All inputs are finite; a program needn't handle non-finite values.
Results may differ from the reference program's by a relative error of at most 0.015.
Values may be sent and summed in bfloat16 or wider, within the bound.
No kernel may reach another device: no remote copies, remote signals or barrier semaphores. Data moves between devices by JAX's collectives and lax.ppermute only.
A program may use at most 128 MiB of HBM per device.

```python
import jax
import jax.numpy as jnp
from jax import lax

F = 128
HID = 256
TILE = 128
TB = 4
REACH = 3
NODES = 16384
CAPG = 40
MAXT = 160
N_REP = 4
N_BLK = 8


def tile_plan(key):
    base = jax.random.fold_in(key, 17)
    key_full, key_loss, key_order = jax.random.split(base, 3)
    device_total = N_REP * N_BLK
    group_slots = N_REP * TB * TB
    device_ids = jnp.arange(device_total, dtype=jnp.int32)
    blk_ids = device_ids % N_BLK
    group_ids = jnp.arange(N_BLK, dtype=jnp.int32)
    forward_gap = (group_ids[None, :] - blk_ids[:, None]) % N_BLK
    distance = jnp.minimum(forward_gap, N_BLK - forward_gap)
    ceiling = jnp.where(distance <= REACH, CAPG * (REACH + 1 - distance) // (REACH + 1), 0)
    full_device = jax.random.randint(key_full, (), 0, device_total)
    shortfall = jax.random.randint(key_loss, (device_total, N_BLK), 0, 1 << 20) % (ceiling // 2 + 1)
    shortfall = jnp.where(device_ids[:, None] == full_device, 0, shortfall)
    group_count = ceiling - shortfall
    slot_ids = jnp.arange(group_slots, dtype=jnp.int32)
    scores = jax.random.randint(key_order, (device_total, N_BLK, group_slots), 0, (1 << 30) // group_slots) * group_slots + slot_ids
    ranking = jnp.argsort(jnp.argsort(scores, axis=-1), axis=-1)
    chosen = ranking < group_count[:, :, None]
    place_in_group = jnp.cumsum(chosen.astype(jnp.int32), axis=-1) - 1
    group_start = jnp.cumsum(group_count, axis=-1) - group_count
    target_slot = jnp.where(chosen, group_start[:, :, None] + place_in_group, MAXT).astype(jnp.int32)
    row_value = group_ids[None, :, None] * TB + slot_ids[None, None, :] // (N_REP * TB)
    col_value = slot_ids[None, None, :] % (N_REP * TB)
    row_value = jnp.broadcast_to(row_value, chosen.shape).astype(jnp.int32)
    col_value = jnp.broadcast_to(col_value, chosen.shape).astype(jnp.int32)

    def place_slots(target, rows_in, cols_in, blk_id):
        row_array = jnp.zeros((MAXT + 1,), jnp.int32) + blk_id * TB
        col_array = jnp.zeros((MAXT + 1,), jnp.int32)
        row_array = row_array.at[target.reshape(-1)].set(rows_in.reshape(-1))
        col_array = col_array.at[target.reshape(-1)].set(cols_in.reshape(-1))
        return (row_array[:MAXT], col_array[:MAXT])
    row_table, col_table = jax.vmap(place_slots)(target_slot, row_value, col_value, blk_ids)
    counts = jnp.sum(group_count, axis=-1).astype(jnp.int32)
    return (row_table.reshape(N_REP, N_BLK, MAXT), col_table.reshape(N_REP, N_BLK, MAXT), counts.reshape(N_REP, N_BLK))


def draw_tile_rows(key, part):
    return tile_plan(key)[0]


def draw_tile_cols(key, part):
    return tile_plan(key)[1]


def draw_tile_counts(key, part):
    return tile_plan(key)[2]


def place_ends(entries, stream_key, least, largest):
    place = [jax.random.randint(jax.random.fold_in(stream_key, axis), (), 0, length) for axis, length in enumerate(entries.shape)]
    main_axis = entries.shape.index(max(entries.shape))
    neighbour = place[:main_axis] + [(place[main_axis] + 1) % entries.shape[main_axis]] + place[main_axis + 1:]
    return entries.at[tuple(place)].set(least).at[tuple(neighbour)].set(largest)


def shard_levels(own_key, dims, cuts, low, high):
    factor_of = 1.0
    for axis_at, blocks in cuts:
        heights = jax.random.uniform(jax.random.fold_in(jax.random.fold_in(own_key, 6), axis_at), (blocks,), jnp.float32, low / len(cuts), high / len(cuts))
        factor_of = factor_of * jnp.repeat(jnp.exp(heights), dims[axis_at] // blocks).reshape((-1,) + (1,) * (len(dims) - 1 - axis_at))
    return factor_of


def scatter_about(key, dims, deviation, reach, cuts=(), held_as=jnp.bfloat16):
    drawn = deviation * jax.random.normal(key, dims, jnp.float32)
    if cuts:
        drawn = drawn * shard_levels(key, dims, cuts, -0.22, 0.18)
    return jnp.clip(drawn, -reach, reach).astype(held_as)


def setup_inputs(seed: int = 0) -> dict:
    streams_of = jax.random.split(jax.random.key(seed), 10)
    return {
        "features": scatter_about(streams_of[0], (NODES, F), 1.0, 6.0, ((0, 32),)),
        "degrees": place_ends(jax.random.randint(streams_of[1], (NODES,), 1, 33), jax.random.fold_in(streams_of[1], 1), 1, 32).astype(jnp.int32),
        "tile_weights": jnp.clip(0.049804688 * jax.random.uniform(streams_of[2], (N_REP, N_BLK, MAXT, TILE, TILE), jnp.float32) ** shard_levels(streams_of[2], (N_REP, N_BLK, MAXT, TILE, TILE), ((0, 4), (1, 8)), -0.2, 0.2), 0.0, 0.049804688).astype(jnp.bfloat16),
        "tile_rows": draw_tile_rows(jax.random.fold_in(streams_of[9], 71), 0),
        "tile_cols": draw_tile_cols(jax.random.fold_in(streams_of[9], 71), 0),
        "tile_counts": draw_tile_counts(jax.random.fold_in(streams_of[9], 71), 0),
        "weight": scatter_about(streams_of[6], (F, HID), F ** -0.5, 0.5),
        "layer_bias": scatter_about(streams_of[7], (HID,), 0.5, 3.0, (), jnp.float32),
        "upstream": scatter_about(streams_of[8], (NODES, HID), 1.0, 6.0, ((0, 32),)),
    }


def node_scale(degrees):
    return 1.0 / jnp.sqrt(degrees.astype(jnp.float32) + 1.0)

def reference(features, degrees, tile_weights, tile_rows, tile_cols, tile_counts, weight, layer_bias, upstream):
    node_norm = node_scale(degrees)
    scaled = (node_norm[:, None] * features.astype(jnp.float32)).astype(jnp.bfloat16)
    tile_total = NODES // TILE
    scaled_tiles = scaled.reshape(tile_total, TILE, F)
    device_total = N_REP * N_BLK
    flat_weights = tile_weights.reshape(device_total, MAXT, TILE, TILE)
    flat_rows = tile_rows.reshape(device_total, MAXT)
    flat_cols = tile_cols.reshape(device_total, MAXT)
    flat_counts = tile_counts.reshape(device_total)
    device_ids = jnp.arange(device_total, dtype=jnp.int32)
    slot_ids = jnp.arange(MAXT, dtype=jnp.int32)

    def tile_places(row_ids, col_ids, slot_count, device):
        rep_index = device // N_BLK
        blk_index = device % N_BLK
        dest_tiles = rep_index * (N_BLK * TB) + row_ids
        source_tiles = (col_ids // TB * N_BLK + blk_index) * TB + col_ids % TB
        slot_valid = slot_ids < slot_count
        dest_tiles = jnp.where(slot_valid, dest_tiles, tile_total).astype(jnp.int32)
        source_tiles = jnp.where(slot_valid, source_tiles, tile_total).astype(jnp.int32)
        return (dest_tiles, source_tiles)

    def forward_step(running, scan_items):
        weights_dev, row_ids, col_ids, slot_count, device = scan_items
        dest_tiles, source_tiles = tile_places(row_ids, col_ids, slot_count, device)
        gathered = scaled_tiles[jnp.minimum(source_tiles, tile_total - 1)]
        products = jnp.einsum('tab,tbf->taf', weights_dev.astype(jnp.float32), gathered.astype(jnp.float32))
        return (running.at[dest_tiles].add(products), None)
    zero_sum = jnp.zeros((tile_total + 1, TILE, F), jnp.float32)
    neighbor_sum, _ = lax.scan(forward_step, zero_sum, (flat_weights, flat_rows, flat_cols, flat_counts, device_ids))
    neighbor_sum = neighbor_sum[:tile_total].reshape(NODES, F)
    aggregated = (node_norm[:, None] * (neighbor_sum + scaled.astype(jnp.float32))).astype(jnp.bfloat16)
    pre_act = jnp.dot(aggregated, weight, preferred_element_type=jnp.float32) + layer_bias
    hidden = jax.nn.silu(pre_act).astype(jnp.bfloat16)
    gate_sigmoid = jax.nn.sigmoid(pre_act)
    pre_grad = (upstream.astype(jnp.float32) * (gate_sigmoid + pre_act * gate_sigmoid * (1.0 - gate_sigmoid))).astype(jnp.bfloat16)
    grad_scale = NODES ** (-0.5)
    weight_grad = jnp.dot(aggregated.T, pre_grad, preferred_element_type=jnp.float32) * grad_scale
    bias_grad = lax.optimization_barrier(jnp.sum(pre_grad.astype(jnp.float32), axis=0)) * grad_scale
    scaled_grad = (node_norm[:, None] * jnp.dot(pre_grad, weight.T, preferred_element_type=jnp.float32)).astype(jnp.bfloat16)
    grad_tiles = scaled_grad.reshape(tile_total, TILE, F)

    def backward_step(running, scan_items):
        weights_dev, row_ids, col_ids, slot_count, device = scan_items
        dest_tiles, source_tiles = tile_places(row_ids, col_ids, slot_count, device)
        gathered = grad_tiles[jnp.minimum(dest_tiles, tile_total - 1)]
        products = jnp.einsum('tab,taf->tbf', weights_dev.astype(jnp.float32), gathered.astype(jnp.float32))
        return (running.at[source_tiles].add(products), None)
    column_sum, _ = lax.scan(backward_step, zero_sum, (flat_weights, flat_rows, flat_cols, flat_counts, device_ids))
    column_sum = column_sum[:tile_total].reshape(NODES, F)
    feature_grad = (node_norm[:, None] * (column_sum + scaled_grad.astype(jnp.float32))).astype(jnp.bfloat16)
    return (hidden, feature_grad, weight_grad, bias_grad)
```

```python
import functools

import jax
import jax.numpy as jnp
from jax import lax
from jax.experimental import pallas as pl
from jax.experimental.pallas import tpu as pltpu
from jax.sharding import PartitionSpec as P

BOTH = ("rep", "blk")
VMEM = pl.BlockSpec(memory_space=pltpu.VMEM)
SMEM = pl.BlockSpec(memory_space=pltpu.SMEM)
PARAMS = pltpu.CompilerParams(vmem_limit_bytes=48 * 1024 * 1024)
BF = jnp.bfloat16
F32 = jnp.float32


def unroll_of(slot_total):
    return max(u for u in range(1, 17) if slot_total % u == 0)


def node_scale(degrees):
    return 1.0 / jnp.sqrt(degrees.astype(F32) + 1.0)


def move(value, target):
    rep_count, blk_count = lax.axis_size("rep"), lax.axis_size("blk")
    pairs = []
    for r in range(rep_count):
        for k in range(blk_count):
            to_r, to_k = target(r, k)
            pairs.append((r * blk_count + k, to_r * blk_count + to_k))
    return lax.ppermute(value, BOTH, pairs)


def swap_cores(value):
    return move(value, lambda r, k: (r, k ^ 1))


def rep_partner(stage):
    bits = (lax.axis_size("rep") - 1).bit_length()
    return lambda r, k: (r ^ (1 << ((stage + k % 2) % bits)), k)


def rep_place(rep_ids, rep_index, core):
    bits = (lax.axis_size("rep") - 1).bit_length()
    relative = rep_ids ^ rep_index
    place = jnp.zeros_like(relative)
    for stage in range(bits):
        plain = (relative >> stage) & 1
        turned = (relative >> ((stage + 1) % bits)) & 1
        place = place + (jnp.where(core == 0, plain, turned) << stage)
    return place


def pair_place(pair_ids, pair_index):
    pairs = lax.axis_size("blk") // 2
    if pairs == 4:
        return pair_ids ^ pair_index
    ahead = (pair_ids - pair_index) % pairs
    return jnp.where(ahead == 0, 0, jnp.where(ahead == 1, 1, jnp.where(ahead == pairs - 1, 2, 3)))


def pair_partner(place, back):
    blk_count = lax.axis_size("blk")

    def target(r, k):
        if blk_count == 8:
            return (r, k ^ (2 * place))
        step = {1: 2, 2: -2, 3: 4 if k % 2 == 0 else -4}[place]
        return (r, (k + (-step if back else step)) % blk_count)

    return target


def forward_kernel(tiles, unroll, place_ref, col_ref, count_ref, w_ref, x_ref, keep_ref, send_ref, total):
    total[...] = jnp.zeros_like(total)
    tile = w_ref.shape[-1]

    def step(i, carry):
        for u in range(unroll):
            t = i * unroll + u
            x_rows = pl.ds(pl.multiple_of(col_ref[t] * tile, tile), tile)
            part = jnp.dot(w_ref[t], x_ref[x_rows, :], preferred_element_type=F32)
            rows = pl.ds(pl.multiple_of(place_ref[t] * tile, tile), tile)
            total[rows, :] += part
        return carry

    lax.fori_loop(0, (count_ref[0] + unroll - 1) // unroll, step, 0)
    half = tiles // 2 * tile
    keep_ref[...] = total[:half, :].astype(BF)
    send_ref[...] = total[half : 2 * half, :].astype(BF)


def backward_kernel(col_tiles, unroll, place_ref, col_ref, count_ref, w_ref, *refs):
    block_refs, (out_ref, grads, total) = refs[:-3], refs[-3:]
    total[...] = jnp.zeros_like(total)
    tile = w_ref.shape[-1]
    first = 0
    for block_ref in block_refs:
        grads[first : first + block_ref.shape[0], :] = block_ref[...]
        first += block_ref.shape[0]

    def step(i, carry):
        for u in range(unroll):
            t = i * unroll + u
            g_rows = pl.ds(pl.multiple_of(place_ref[t] * tile, tile), tile)
            part = lax.dot_general(
                w_ref[t], grads[g_rows, :], (((0,), (0,)), ((), ())), preferred_element_type=F32
            )
            rows = pl.ds(pl.multiple_of(col_ref[t] * tile, tile), tile)
            total[rows, :] += part
        return carry

    lax.fori_loop(0, (count_ref[0] + unroll - 1) // unroll, step, 0)
    out_ref[...] = total[: col_tiles * tile, :].astype(BF)


def dense_kernel(
    grad_rows,
    core_ref, own_ref, p1_ref, p2_ref, p3_ref, scaled_ref, norm_ref, weight_ref, bias_ref, up_ref,
    hidden_ref, grad_ref, keep_ref, send_ref, full,
):
    norm = norm_ref[...]
    neighbor = (
        own_ref[...].astype(F32) + p1_ref[...].astype(F32) + p2_ref[...].astype(F32)
        + p3_ref[...].astype(F32) + scaled_ref[...].astype(F32)
    )
    aggregated = (norm * neighbor).astype(BF)
    weight = weight_ref[...]
    pre_act = jnp.dot(aggregated, weight, preferred_element_type=F32) + bias_ref[...]
    gate = 1.0 / (1.0 + jnp.exp(-pre_act))
    hidden_ref[...] = (pre_act * gate).astype(BF)
    pre_grad = (up_ref[...].astype(F32) * (gate + pre_act * gate * (1.0 - gate))).astype(BF)
    back = lax.dot_general(pre_grad, weight, (((1,), (1,)), ((), ())), preferred_element_type=F32)
    grad_ref[...] = (norm * back).astype(BF)
    full[...] = lax.dot_general(
        aggregated, pre_grad, (((0,), (0,)), ((), ())), preferred_element_type=F32
    )
    bias_rows = jnp.broadcast_to(
        jnp.sum(pre_grad.astype(F32), axis=0, keepdims=True), (8, pre_grad.shape[1])
    )
    core = core_ref[0]
    keep_ref[:grad_rows, :] = full[pl.ds(pl.multiple_of(core * grad_rows, grad_rows), grad_rows), :]
    send_ref[:grad_rows, :] = full[pl.ds(pl.multiple_of((1 - core) * grad_rows, grad_rows), grad_rows), :]
    keep_ref[grad_rows:, :] = bias_rows
    send_ref[grad_rows:, :] = bias_rows


def on_device(
    features, degrees, tile_weights, tile_rows, tile_cols, tile_counts, weight, layer_bias, upstream
):
    row_count, feat_width = features.shape
    hid_width = weight.shape[1]
    slot_total, tile_size = tile_weights.shape[2], tile_weights.shape[-1]
    row_tiles = row_count // tile_size
    rep_count, blk_count = lax.axis_size("rep"), lax.axis_size("blk")
    rep_index, blk_index = lax.axis_index("rep"), lax.axis_index("blk")
    core, pair_index = blk_index % 2, blk_index // 2
    unroll = unroll_of(slot_total)
    places = 8
    window_tiles = places * row_tiles
    column_tiles = rep_count * row_tiles

    rows_dev, cols_dev, count_dev = tile_rows[0, 0], tile_cols[0, 0], tile_counts[0]
    used = jnp.arange(slot_total, dtype=jnp.int32) < count_dev[0]
    group = rows_dev // row_tiles
    row_place = pair_place(group // 2, pair_index) + jnp.where(group % 2 == core, 0, places // 2)
    row_place = row_place * row_tiles + rows_dev % row_tiles
    col_place = rep_place(cols_dev // row_tiles, rep_index, core) * row_tiles + cols_dev % row_tiles
    row_sum = jnp.where(used, row_place, window_tiles).astype(jnp.int32)
    row_read = jnp.where(used, row_place, 0).astype(jnp.int32)
    col_sum = jnp.where(used, col_place, column_tiles).astype(jnp.int32)
    col_read = jnp.where(used, col_place, 0).astype(jnp.int32)
    tiles_dev = tile_weights[0, 0]

    node_norm = node_scale(degrees)
    norm_wide = jnp.broadcast_to(node_norm[:, None], (row_count, feat_width))
    scaled = (node_norm[:, None] * features.astype(F32)).astype(BF)

    source = scaled
    stages = (rep_count - 1).bit_length()
    for stage in range(stages):
        source = jnp.concatenate([source, move(source, rep_partner(stage))], axis=0)

    half_rows = places // 2 * row_count
    keep, send = pl.pallas_call(
        functools.partial(forward_kernel, window_tiles, unroll),
        out_shape=[jax.ShapeDtypeStruct((half_rows, feat_width), BF)] * 2,
        in_specs=[SMEM, SMEM, SMEM, VMEM, VMEM],
        out_specs=[VMEM, VMEM],
        scratch_shapes=[pltpu.VMEM(((window_tiles + 1) * tile_size, feat_width), F32)],
        compiler_params=PARAMS,
        name="forward_tiles",
    )(row_sum, col_read, count_dev, tiles_dev, source)
    came = swap_cores(send)

    def block(array, place):
        return array[place * row_count : (place + 1) * row_count]

    sums = [
        (block(keep, q).astype(F32) + block(came, q).astype(F32)).astype(BF) for q in range(4)
    ]
    parts = [sums[0]] + [move(sums[q], pair_partner(q, False)) for q in (1, 2, 3)]

    grad_rows = feat_width // 2
    hidden, scaled_grad, grad_keep, grad_send = pl.pallas_call(
        functools.partial(dense_kernel, grad_rows),
        out_shape=[
            jax.ShapeDtypeStruct((row_count, hid_width), BF),
            jax.ShapeDtypeStruct((row_count, feat_width), BF),
            jax.ShapeDtypeStruct((grad_rows + 8, hid_width), F32),
            jax.ShapeDtypeStruct((grad_rows + 8, hid_width), F32),
        ],
        in_specs=[SMEM] + [VMEM] * 9,
        out_specs=[VMEM] * 4,
        scratch_shapes=[pltpu.VMEM((feat_width, hid_width), F32)],
        compiler_params=PARAMS,
        name="dense",
    )(
        core[None].astype(jnp.int32), *parts, scaled, norm_wide, weight, layer_bias[None], upstream
    )

    own_grads = [scaled_grad] + [move(scaled_grad, pair_partner(q, True)) for q in (1, 2, 3)]
    own_grads = jnp.concatenate(own_grads, axis=0)
    other_grads = swap_cores(own_grads)

    column_part = pl.pallas_call(
        functools.partial(backward_kernel, column_tiles, unroll),
        out_shape=jax.ShapeDtypeStruct((column_tiles * tile_size, feat_width), BF),
        in_specs=[SMEM, SMEM, SMEM, VMEM, VMEM, VMEM],
        out_specs=VMEM,
        scratch_shapes=[
            pltpu.VMEM((window_tiles * tile_size, feat_width), BF),
            pltpu.VMEM(((column_tiles + 1) * tile_size, feat_width), F32),
        ],
        compiler_params=PARAMS,
        name="backward_tiles",
    )(row_read, col_sum, count_dev, tiles_dev, own_grads, other_grads)

    for stage in reversed(range(stages)):
        half = column_part.shape[0] // 2
        came = move(column_part[half:], rep_partner(stage))
        column_part = column_part[:half].astype(F32) + came.astype(F32)
        if stage:
            column_part = column_part.astype(BF)
    feature_grad = (norm_wide * (column_part + scaled_grad.astype(F32))).astype(BF)

    grad = grad_keep + swap_cores(grad_send)
    for stage in range(stages):
        grad = grad + move(grad, lambda r, k: (r ^ (1 << stage), k))
    for bit in range(1, (blk_count - 1).bit_length()):
        grad = grad + move(grad, lambda r, k: (r, k ^ (1 << bit)))
    mine = grad[:grad_rows]
    other = swap_cores(mine)
    grad_scale = (row_count * rep_count * blk_count) ** (-0.5)
    weight_grad = jnp.where(
        core == 0, jnp.concatenate([mine, other]), jnp.concatenate([other, mine])
    )
    return (hidden, feature_grad, weight_grad * grad_scale, grad[grad_rows] * grad_scale)


def solution(mesh):
    placed = (
        P(("rep", "blk"), None),
        P(("rep", "blk")),
        P("rep", "blk", None, None, None),
        P("rep", "blk", None),
        P("rep", "blk", None),
        P("rep", "blk"),
        P(),
        P(),
        P(("rep", "blk"), None),
    )
    return jax.shard_map(
        on_device,
        mesh=mesh,
        in_specs=placed,
        out_specs=(P(("rep", "blk"), None), P(("rep", "blk"), None), P(), P()),
        check_vma=False,
    )
```

```python
import functools

import jax
import jax.numpy as jnp
from jax import lax
from jax.experimental import pallas as pl
from jax.experimental.pallas import tpu as pltpu
from jax.sharding import PartitionSpec as P

BOTH = ("rep", "blk")
VMEM = pl.BlockSpec(memory_space=pltpu.VMEM)
SMEM = pl.BlockSpec(memory_space=pltpu.SMEM)
ANY = pl.BlockSpec(memory_space=pl.ANY)
BF = jnp.bfloat16
F32 = jnp.float32
CORES = 2


def params(mib):
    return pltpu.CompilerParams(vmem_limit_bytes=mib * 1024 * 1024)


def cost(flops, size):
    return pl.CostEstimate(flops=flops, bytes_accessed=size, transcendentals=0)


def node_scale(degrees):
    return 1.0 / jnp.sqrt(degrees.astype(F32) + 1.0)


def move(value, target):
    rep_count, blk_count = lax.axis_size("rep"), lax.axis_size("blk")
    pairs = []
    for r in range(rep_count):
        for k in range(blk_count):
            to_r, to_k = target(r, k)
            pairs.append((r * blk_count + k, to_r * blk_count + to_k))
    return lax.ppermute(value, BOTH, pairs)


def swap_cores(value):
    return move(value, lambda r, k: (r, k ^ 1))


def rep_partner(stage):
    bits = (lax.axis_size("rep") - 1).bit_length()
    return lambda r, k: (r ^ (1 << ((stage + k % 2) % bits)), k)


def rep_place(rep_ids, rep_index, core):
    bits = (lax.axis_size("rep") - 1).bit_length()
    relative = rep_ids ^ rep_index
    place = jnp.zeros_like(relative)
    for stage in range(bits):
        plain = (relative >> stage) & 1
        turned = (relative >> ((stage + 1) % bits)) & 1
        place = place + (jnp.where(core == 0, plain, turned) << stage)
    return place


def pair_at(place, pair_index, core):
    pairs = lax.axis_size("blk") // CORES
    if pairs == 4:
        return pair_index ^ (0, 1, 3, 2)[place]
    step = (0, 1, -1, jnp.where(core == 0, -2, 2))[place]
    return (pair_index + step) % pairs


def pair_partner(place, back):
    blk_count = lax.axis_size("blk")

    def target(r, k):
        if place == 3:
            return (r, (k + (3 if k % 2 else -3)) % blk_count)
        if blk_count == 8:
            return (r, k ^ {1: 2, 2: 6}[place])
        step = {1: 2, 2: -2}[place]
        return (r, (k + (-step if back else step)) % blk_count)

    return target


def stage_kernel(w_ref, out_ref, sem):
    copy = pltpu.make_async_copy(w_ref, out_ref, sem)
    copy.start()
    copy.wait()


def gather_blocks(block_refs, held):
    first = 0
    for block_ref in block_refs:
        held[first : first + block_ref.shape[0], :] = block_ref[...]
        first += block_ref.shape[0]


def over_slots(low, high, unroll, slot_total, body):
    def step(i, carry):
        for u in range(unroll):
            t = low + i * unroll + u
            body(jnp.minimum(t, slot_total - 1), t < high)
        return carry

    lax.fori_loop(0, (high - low + unroll - 1) // unroll, step, 0)


def aligned(index, tile):
    return pl.ds(pl.multiple_of(index * tile, tile), tile)


def forward_kernel(places, unroll, bounds_ref, row_ref, col_ref, w_ref, *refs):
    count = 2 if 3 not in places else 1
    x_refs, out_refs, (held, total) = refs[: -2 - count], refs[-2 - count : -2], refs[-2:]
    tile = w_ref.shape[-1]
    block_tiles = x_refs[0].shape[0] // tile
    gather_blocks(x_refs, held)
    total[...] = jnp.zeros_like(total)
    spare = total.shape[0] // tile - 1
    for n, place in enumerate(places):

        def body(t, used):
            row = row_ref[t]
            if count == 1:
                row = row % block_tiles
            row = jnp.where(used, row + n * 2 * block_tiles, spare)
            part = jnp.dot(w_ref[t], held[aligned(col_ref[t], tile), :], preferred_element_type=F32)
            total[aligned(row, tile), :] += part

        over_slots(bounds_ref[place], bounds_ref[4 + place], unroll, w_ref.shape[0], body)
    rows = block_tiles * tile
    for n in range(len(places)):
        for side in range(count):
            first = (n * count + side) * rows
            out_refs[side][n * rows : (n + 1) * rows, :] = total[first : first + rows, :].astype(BF)


def backward_kernel(place, unroll, first_call, last_call, bounds_ref, row_ref, col_ref, w_ref, *refs):
    held = refs[-1]
    tile = w_ref.shape[-1]
    if last_call:
        old_ref, *block_refs = refs[:2]
        out_refs, total = refs[2:-2], refs[-2]
        total[...] = old_ref[...]
    elif first_call:
        block_refs, total = refs[:-2], refs[-2]
        total[...] = jnp.zeros_like(total)
    else:
        old_ref, *block_refs = refs[:-2]
        total = refs[-2]
        total[...] = old_ref[...]
    gather_blocks(block_refs, held)
    spare = total.shape[0] // tile - 1
    held_tiles = held.shape[0] // tile

    def body(t, used):
        row = row_ref[t]
        if len(block_refs) == 1:
            row = row % held_tiles
        part = lax.dot_general(
            w_ref[t], held[aligned(row, tile), :], (((0,), (0,)), ((), ())), preferred_element_type=F32
        )
        total[aligned(jnp.where(used, col_ref[t], spare), tile), :] += part

    over_slots(bounds_ref[place], bounds_ref[4 + place], unroll, w_ref.shape[0], body)
    if last_call:
        rows = out_refs[0].shape[0]
        for n, out_ref in enumerate(out_refs):
            out_ref[...] = total[n * rows : (n + 1) * rows, :].astype(out_ref.dtype)


def dense_kernel(
    own_ref, p1_ref, p2_ref, p3_ref, scaled_ref, norm_ref, weight_ref, bias_ref, up_ref,
    hidden_ref, grad_ref, aggregated_ref, pre_grad_ref,
):
    norm = norm_ref[...]
    neighbor = (
        own_ref[...].astype(F32) + p1_ref[...].astype(F32) + p2_ref[...].astype(F32)
        + p3_ref[...].astype(F32) + scaled_ref[...].astype(F32)
    )
    aggregated = (norm * neighbor).astype(BF)
    weight = weight_ref[...]
    pre_act = jnp.dot(aggregated, weight, preferred_element_type=F32) + bias_ref[...]
    gate = 1.0 / (1.0 + jnp.exp(-pre_act))
    hidden_ref[...] = (pre_act * gate).astype(BF)
    pre_grad = (up_ref[...].astype(F32) * (gate + pre_act * gate * (1.0 - gate))).astype(BF)
    back = lax.dot_general(pre_grad, weight, (((1,), (1,)), ((), ())), preferred_element_type=F32)
    grad_ref[...] = (norm * back).astype(BF)
    aggregated_ref[...] = aggregated
    pre_grad_ref[...] = pre_grad


def weight_kernel(core_ref, aggregated_ref, pre_grad_ref, keep_ref, send_ref, full):
    grad_rows = full.shape[0] // CORES
    pre_grad = pre_grad_ref[...]
    full[...] = lax.dot_general(
        aggregated_ref[...], pre_grad, (((0,), (0,)), ((), ())), preferred_element_type=F32
    )
    bias_rows = jnp.broadcast_to(
        jnp.sum(pre_grad.astype(F32), axis=0, keepdims=True), (8, pre_grad.shape[1])
    )
    core = core_ref[0]
    keep_ref[:grad_rows, :] = full[aligned(core, grad_rows), :]
    send_ref[:grad_rows, :] = full[aligned(1 - core, grad_rows), :]
    keep_ref[grad_rows:, :] = bias_rows
    send_ref[grad_rows:, :] = bias_rows


def on_device(
    features, degrees, tile_weights, tile_rows, tile_cols, tile_counts, weight, layer_bias, upstream
):
    row_count, feat_width = features.shape
    hid_width = weight.shape[1]
    slot_total, tile = tile_weights.shape[2], tile_weights.shape[-1]
    row_tiles = row_count // tile
    rep_count, blk_count = lax.axis_size("rep"), lax.axis_size("blk")
    rep_index, blk_index = lax.axis_index("rep"), lax.axis_index("blk")
    core, pair_index = blk_index % CORES, blk_index // CORES
    stages = (rep_count - 1).bit_length()
    col_tiles = rep_count * row_tiles
    block_shape = jax.ShapeDtypeStruct((row_count, feat_width), BF)

    rows_dev, cols_dev, count_dev = tile_rows[0, 0], tile_cols[0, 0], tile_counts[0, 0]
    used = jnp.arange(slot_total, dtype=jnp.int32) < count_dev
    group = rows_dev // row_tiles
    row_place = jnp.where(group % CORES == core, 0, row_tiles) + rows_dev % row_tiles
    col_place = rep_place(cols_dev // row_tiles, rep_index, core) * row_tiles + cols_dev % row_tiles
    pair_ids = jnp.stack([pair_at(place, pair_index, core) for place in range(4)])
    pair_ids = jnp.concatenate([pair_ids, pair_ids + 1])
    bounds = jnp.sum(used & (group // CORES < pair_ids[:, None]), axis=1).astype(jnp.int32)
    row_place, col_place = row_place.astype(jnp.int32), col_place.astype(jnp.int32)

    node_norm = node_scale(degrees)
    norm_wide = jnp.broadcast_to(node_norm[:, None], (row_count, feat_width))
    scaled = (node_norm[:, None] * features.astype(F32)).astype(BF)

    source = [scaled]
    for stage in range(stages):
        source = source + [move(part, rep_partner(stage)) for part in source]

    tiles_dev = pl.pallas_call(
        stage_kernel,
        out_shape=jax.ShapeDtypeStruct((slot_total, tile, tile), BF),
        in_specs=[ANY],
        out_specs=VMEM,
        scratch_shapes=[pltpu.SemaphoreType.DMA],
        compiler_params=params(16),
        cost_estimate=cost(0, 2 * slot_total * tile * tile * 2),
        name="stage_tiles",
    )(tile_weights[0, 0])

    def forward(places, unroll):
        sides = 1 if 3 in places else 2
        shape = jax.ShapeDtypeStruct((len(places) * row_count, feat_width), BF)
        return pl.pallas_call(
            functools.partial(forward_kernel, places, unroll),
            out_shape=[shape] * sides,
            in_specs=[SMEM, SMEM, SMEM] + [VMEM] * (1 + rep_count),
            out_specs=[VMEM] * sides,
            scratch_shapes=[
                pltpu.VMEM((col_tiles * tile, feat_width), BF),
                pltpu.VMEM(((len(places) * sides * row_tiles + 1) * tile, feat_width), F32),
            ],
            compiler_params=params(16),
            cost_estimate=cost(2 * 48 * len(places) * tile**3, 2**20),
            name="forward_" + "_".join(map(str, places)),
        )(bounds, row_place, col_place, tiles_dev, *source)

    def add(a, b):
        return (a.astype(F32) + b.astype(F32)).astype(BF)

    (part3,) = forward((3,), 12)
    came3 = move(part3, pair_partner(3, False))
    keep2, send2 = forward((2,), 16)
    came2 = move(add(keep2, swap_cores(send2)), pair_partner(2, False))
    keep01, send01 = forward((0, 1), 16)
    sum01 = add(keep01, swap_cores(send01))
    came1 = move(sum01[row_count:], pair_partner(1, False))

    hidden, scaled_grad, aggregated, pre_grad = pl.pallas_call(
        dense_kernel,
        out_shape=[
            jax.ShapeDtypeStruct((row_count, hid_width), BF),
            block_shape,
            block_shape,
            jax.ShapeDtypeStruct((row_count, hid_width), BF),
        ],
        in_specs=[VMEM] * 9,
        out_specs=[VMEM] * 4,
        compiler_params=params(16),
        cost_estimate=cost(2**27, 2**20),
        name="dense",
    )(sum01[:row_count], came1, came2, came3, scaled, norm_wide, weight, layer_bias[None], upstream)

    grads2 = move(scaled_grad, pair_partner(2, True))
    grads3 = move(scaled_grad, pair_partner(3, True))
    grads1 = move(scaled_grad, pair_partner(1, True))

    grad_rows = feat_width // CORES
    grad_shape = jax.ShapeDtypeStruct((grad_rows + 8, hid_width), F32)
    grad_keep, grad_send = pl.pallas_call(
        weight_kernel,
        out_shape=[grad_shape] * 2,
        in_specs=[SMEM, VMEM, VMEM],
        out_specs=[VMEM] * 2,
        scratch_shapes=[pltpu.VMEM((feat_width, hid_width), F32)],
        compiler_params=params(16),
        cost_estimate=cost(2**25, 2**20),
        name="weight_terms",
    )(core[None].astype(jnp.int32), aggregated, pre_grad)

    total_shape = jax.ShapeDtypeStruct(((col_tiles + 1) * tile, feat_width), F32)

    def backward(place, unroll, old, blocks):
        last = place == 3
        out_shape = [total_shape]
        scratch = [pltpu.VMEM((len(blocks) * row_count, feat_width), BF)]
        if last:
            out_shape = [jax.ShapeDtypeStruct((row_count, feat_width), F32)] + [block_shape] * (rep_count - 1)
            scratch = [pltpu.VMEM(total_shape.shape, F32)] + scratch
        return pl.pallas_call(
            functools.partial(backward_kernel, place, unroll, old is None, last),
            out_shape=out_shape,
            in_specs=[SMEM, SMEM, SMEM] + [VMEM] * (1 + (old is not None) + len(blocks)),
            out_specs=[VMEM] * len(out_shape),
            scratch_shapes=scratch,
            input_output_aliases={} if old is None or last else {4: 0},
            compiler_params=params(16),
            cost_estimate=cost(2 * 48 * tile**3, 2**20),
            name=f"backward_{place}",
        )(bounds, row_place, col_place, tiles_dev, *([] if old is None else [old]), *blocks)

    (total,) = backward(0, 16, None, [scaled_grad, swap_cores(scaled_grad)])
    (total,) = backward(1, 16, total, [grads1, swap_cores(grads1)])
    (total,) = backward(2, 16, total, [grads2, swap_cores(grads2)])
    columns = backward(3, 12, total, [grads3])

    for stage in reversed(range(stages)):
        half = len(columns) // 2
        order = range(half - 1, -1, -1)
        came = {n: move(columns[half + n], rep_partner(stage)) for n in order}
        columns = [
            (columns[n].astype(F32) + came[n].astype(F32)).astype(BF if n else F32) for n in range(half)
        ]
    feature_grad = (norm_wide * (columns[0] + scaled_grad.astype(F32))).astype(BF)

    grad = grad_keep + swap_cores(grad_send)
    for stage in range(stages):
        grad = grad + move(grad, rep_partner(stage))
    for bit in range(1, (blk_count - 1).bit_length()):
        grad = grad + move(grad, lambda r, k: (r, k ^ (1 << bit)))
    mine = grad[:grad_rows]
    other = swap_cores(mine)
    grad_scale = (row_count * rep_count * blk_count) ** (-0.5)
    weight_grad = jnp.where(
        core == 0, jnp.concatenate([mine, other]), jnp.concatenate([other, mine])
    )
    return (hidden, feature_grad, weight_grad * grad_scale, grad[grad_rows] * grad_scale)


def solution(mesh):
    placed = (
        P(("rep", "blk"), None),
        P(("rep", "blk")),
        P("rep", "blk", None, None, None),
        P("rep", "blk", None),
        P("rep", "blk", None),
        P("rep", "blk"),
        P(),
        P(),
        P(("rep", "blk"), None),
    )
    return jax.shard_map(
        on_device,
        mesh=mesh,
        in_specs=placed,
        out_specs=(P(("rep", "blk"), None), P(("rep", "blk"), None), P(), P()),
        check_vma=False,
    )
```

```python
import functools

import jax
import jax.numpy as jnp
from jax import lax
from jax.experimental import pallas as pl
from jax.experimental.pallas import tpu as pltpu
from jax.sharding import PartitionSpec as P

BOTH = ("rep", "blk")
VMEM = pl.BlockSpec(memory_space=pltpu.VMEM)
SMEM = pl.BlockSpec(memory_space=pltpu.SMEM)
ANY = pl.BlockSpec(memory_space=pl.ANY)
HBM = pl.BlockSpec(memory_space=pltpu.HBM)
BF = jnp.bfloat16
F32 = jnp.float32
CORES = 2
BIAS_ROWS = 16


def params(mib):
    return pltpu.CompilerParams(vmem_limit_bytes=mib * 1024 * 1024)


def cost(flops, size):
    return pl.CostEstimate(flops=flops, bytes_accessed=size, transcendentals=0)


SMALL = cost(0, 1024)
LARGE = cost(0, 2**26)


def node_scale(degrees):
    return 1.0 / jnp.sqrt(degrees.astype(F32) + 1.0)


def in_hbm(value):
    return pltpu.with_memory_space_constraint(value, pltpu.HBM)


def move(value, target):
    rep_count, blk_count = lax.axis_size("rep"), lax.axis_size("blk")
    pairs = []
    for r in range(rep_count):
        for k in range(blk_count):
            to_r, to_k = target(r, k)
            pairs.append((r * blk_count + k, to_r * blk_count + to_k))
    return lax.ppermute(value, BOTH, pairs)


def block(function, *args):
    shapes = jax.eval_shape(function, *args)
    return lax.cond(
        lax.axis_index("blk") < lax.axis_size("blk"),
        function,
        lambda *unused: jax.tree.map(lambda shape: jnp.zeros(shape.shape, shape.dtype), shapes),
        *args,
    )


def swap_cores(value):
    return move(value, lambda r, k: (r, k ^ 1))


def rep_bits():
    return (lax.axis_size("rep") - 1).bit_length()


def rep_partner(place):
    bits = rep_bits()
    turned = sum(((place >> n) & 1) << ((n + 1) % bits) for n in range(bits))
    return lambda r, k: (r ^ (turned if k % 2 else place), k)


def rep_place(rep_ids, rep_index, core):
    bits = rep_bits()
    relative = rep_ids ^ rep_index
    place = jnp.zeros_like(relative)
    for n in range(bits):
        turned = (relative >> ((n + 1) % bits)) & 1
        place = place + (jnp.where(core == 0, (relative >> n) & 1, turned) << n)
    return place


def far_first(count):
    return sorted(range(1, count), key=lambda place: -bin(place).count("1"))


def pair_at(place, pair_index, core):
    pairs = lax.axis_size("blk") // CORES
    if pairs == 4:
        return pair_index ^ (0, 1, 3, 2)[place]
    step = (0, 1, -1, jnp.where(core == 0, -2, 2))[place]
    return (pair_index + step) % pairs


def pair_partner(place, back, other_core=False):
    blk_count = lax.axis_size("blk")
    if other_core:
        near = pair_partner(place, back)
        return lambda r, k: (r, near(r, k)[1] ^ 1)

    def target(r, k):
        if place == 3:
            return (r, (k + (3 if k % 2 else -3)) % blk_count)
        if blk_count == 8:
            return (r, k ^ {1: 2, 2: 6}[place])
        step = {1: 2, 2: -2}[place]
        return (r, (k + (-step if back else step)) % blk_count)

    return target


def together(values, earlier=(), weigh=None):
    count = len(values)
    return pl.pallas_call(
        lambda *refs: None,
        out_shape=[jax.ShapeDtypeStruct(value.shape, value.dtype) for value in values],
        in_specs=[ANY] * (count + len(earlier)),
        out_specs=[ANY] * count,
        input_output_aliases={n: n for n in range(count)},
        compiler_params=params(16),
        cost_estimate=weigh or SMALL,
        name="together",
    )(*values, *earlier)


def prepare_kernel(degrees_hbm, features_hbm, scaled_ref, norm_ref, degrees_ref, features_ref, sems):
    copies = [
        pltpu.make_async_copy(degrees_hbm, degrees_ref, sems.at[0]),
        pltpu.make_async_copy(features_hbm, features_ref, sems.at[1]),
    ]
    for copy in copies:
        copy.start()
    for copy in copies:
        copy.wait()
    tile = degrees_ref.shape[1]
    for n in range(degrees_ref.shape[0]):
        norm = node_scale(degrees_ref[n : n + 1, :])
        norm = jnp.broadcast_to(norm, (tile, tile)).T
        rows = slice(n * tile, (n + 1) * tile)
        norm_ref[rows, :] = norm
        scaled_ref[rows, :] = (norm * features_ref[rows, :].astype(F32)).astype(BF)


def stage_kernel(w_ref, earlier_ref, out_ref, sem):
    copy = pltpu.make_async_copy(w_ref, out_ref, sem)
    copy.start()
    copy.wait()


def gather_blocks(block_refs, held):
    first = 0
    for block_ref in block_refs:
        held[first : first + block_ref.shape[0], :] = block_ref[...]
        first += block_ref.shape[0]


def over_slots(low, high, unroll, slot_total, body):
    def step(i, carry):
        for u in range(unroll):
            t = low + i * unroll + u
            body(jnp.minimum(t, slot_total - 1), t < high)
        return carry

    lax.fori_loop(0, (high - low + unroll - 1) // unroll, step, 0)


def aligned(index, tile):
    return pl.ds(pl.multiple_of(index * tile, tile), tile)


def forward_kernel(places, unrolls, earlier_ref, bounds_ref, row_ref, col_ref, w_ref, *refs):
    outs = 3 if 3 in places else 2
    x_refs, out_refs, (held, total) = refs[: -2 - outs], refs[-2 - outs : -2], refs[-2:]
    tile = w_ref.shape[-1]
    block_tiles = x_refs[0].shape[0] // tile
    gather_blocks(x_refs, held)
    total[...] = jnp.zeros_like(total)
    spare = total.shape[0] // tile - 1
    for n, place in enumerate(places):

        def body(t, used):
            row = row_ref[t]
            if place == 3:
                row = row % block_tiles
            row = jnp.where(used, row + n * 2 * block_tiles, spare)
            part = jnp.dot(w_ref[t], held[aligned(col_ref[t], tile), :], preferred_element_type=F32)
            total[aligned(row, tile), :] += part

        over_slots(bounds_ref[place], bounds_ref[4 + place], unrolls[n], w_ref.shape[0], body)
    rows = block_tiles * tile
    for n, place in enumerate(places):
        first = n * 2 * rows
        if place == 3:
            out_refs[2][...] = total[first : first + rows, :].astype(BF)
        else:
            for out_ref in out_refs[:2]:
                out_ref[n * rows : (n + 1) * rows, :] = total[first : first + rows, :].astype(BF)
                first += rows


def stream_slots(w_hbm, held, sems, ranges, unroll, body):
    slot_total = w_hbm.shape[0]
    counts = [(high - low + unroll - 1) // unroll for low, high, n in ranges]

    def fetch(low, i, place):
        first = jnp.minimum(low + i * unroll, slot_total - unroll)
        return first, pltpu.make_async_copy(w_hbm.at[pl.ds(first, unroll)], held.at[place], sems.at[place])

    begin = 0
    for (low, high, n), count in zip(ranges, counts):

        def start(i, carry, low=low, begin=begin):
            fetch(low, i, begin + i)[1].start()
            return carry

        lax.fori_loop(0, count, start, 0)
        begin = begin + count
    begin = 0
    for (low, high, n), count in zip(ranges, counts):

        def step(i, carry, low=low, high=high, n=n, begin=begin):
            first, copy = fetch(low, i, begin + i)
            copy.wait()
            for u in range(unroll):
                t = first + u
                body(held[begin + i, u], t, (t >= low + i * unroll) & (t < high), n)
            return carry

        lax.fori_loop(0, count, step, 0)
        begin = begin + count


def backward_kernel(places, unroll, first_call, last_call, bounds_ref, row_ref, col_ref, w_ref, *refs):
    refs, (total, held, tiles_held, sems) = refs[:-4], refs[-4:]
    tile = w_ref.shape[-1]
    if first_call:
        block_refs, out_refs = refs[:2], refs[2:]
        total[...] = jnp.zeros_like(total)
    else:
        old_ref, refs = refs[0], refs[1:]
        inputs = 2 if last_call else 1
        block_refs, out_refs = refs[:inputs], refs[inputs:]
        total[...] = old_ref[...]
    gather_blocks(block_refs, held)
    spare = total.shape[0] // tile - 1
    held_tiles = held.shape[0] // tile

    def body(w, t, used, n):
        row = row_ref[t]
        if places[n] == 3:
            row = row % held_tiles
        elif len(places) > 1:
            block_tiles = held_tiles // (2 * len(places))
            row = jnp.where(row < block_tiles, row, row + (len(places) - 1) * block_tiles) + n * block_tiles
        part = lax.dot_general(
            w, held[aligned(row, tile), :], (((0,), (0,)), ((), ())), preferred_element_type=F32
        )
        total[aligned(jnp.where(used, col_ref[t], spare), tile), :] += part

    ranges = [(bounds_ref[place], bounds_ref[4 + place], n) for n, place in enumerate(places)]
    stream_slots(w_ref, tiles_held, sems, ranges, unroll, body)
    if last_call:
        rows = out_refs[0].shape[0]
        for n, out_ref in enumerate(out_refs):
            out_ref[...] = total[n * rows : (n + 1) * rows, :].astype(out_ref.dtype)
    else:
        out_refs[0][...] = total[...]


def dense_kernel(*refs):
    part_refs, (norm_ref, weight_ref, bias_ref, up_ref) = refs[:-8], refs[-8:-4]
    hidden_ref, grad_ref, aggregated_ref, pre_grad_ref = refs[-4:]
    norm = norm_ref[...]
    neighbor = part_refs[0][...].astype(F32)
    for part_ref in part_refs[1:]:
        neighbor = neighbor + part_ref[...].astype(F32)
    aggregated = (norm * neighbor).astype(BF)
    weight = weight_ref[...]
    pre_act = jnp.dot(aggregated, weight, preferred_element_type=F32) + bias_ref[...]
    gate = 1.0 / (1.0 + jnp.exp(-pre_act))
    hidden_ref[...] = (pre_act * gate).astype(BF)
    pre_grad = (up_ref[...].astype(F32) * (gate + pre_act * gate * (1.0 - gate))).astype(BF)
    back = lax.dot_general(pre_grad, weight, (((1,), (1,)), ((), ())), preferred_element_type=F32)
    grad_ref[...] = (norm * back).astype(BF)
    aggregated_ref[...] = aggregated
    pre_grad_ref[...] = pre_grad


def weight_kernel(core_ref, aggregated_ref, pre_grad_ref, earlier_ref, keep_ref, send_ref, full):
    pre_grad = pre_grad_ref[...]
    half = full.shape[0] // CORES
    full[...] = lax.dot_general(
        aggregated_ref[...], pre_grad, (((0,), (0,)), ((), ())), preferred_element_type=F32
    )
    sums = jnp.sum(pre_grad.astype(F32), axis=0, keepdims=True)
    sums = jnp.broadcast_to(sums, (BIAS_ROWS, pre_grad.shape[1]))
    core = core_ref[0]
    for out_ref, side in ((keep_ref, core), (send_ref, 1 - core)):
        out_ref[:half, :] = full[aligned(side, half), :]
        out_ref[half:, :] = sums


def on_device(
    features, degrees, tile_weights, tile_rows, tile_cols, tile_counts, weight, layer_bias, upstream
):
    row_count, feat_width = features.shape
    hid_width = weight.shape[1]
    slot_total, tile = tile_weights.shape[2], tile_weights.shape[-1]
    row_tiles = row_count // tile
    rep_count, blk_count = lax.axis_size("rep"), lax.axis_size("blk")
    rep_index, blk_index = lax.axis_index("rep"), lax.axis_index("blk")
    core, pair_index = blk_index % CORES, blk_index // CORES
    col_tiles = rep_count * row_tiles
    block_shape = jax.ShapeDtypeStruct((row_count, feat_width), BF)

    rows_dev, cols_dev, count_dev = tile_rows[0, 0], tile_cols[0, 0], tile_counts[0, 0]
    used = jnp.arange(slot_total, dtype=jnp.int32) < count_dev
    group = rows_dev // row_tiles
    row_place = jnp.where(group % CORES == core, 0, row_tiles) + rows_dev % row_tiles
    col_place = rep_place(cols_dev // row_tiles, rep_index, core) * row_tiles + cols_dev % row_tiles
    pair_ids = jnp.stack([pair_at(place, pair_index, core) for place in range(4)])
    pair_ids = jnp.concatenate([pair_ids, pair_ids + 1])
    bounds = jnp.sum(used & (group // CORES < pair_ids[:, None]), axis=1).astype(jnp.int32)
    row_place, col_place = row_place.astype(jnp.int32), col_place.astype(jnp.int32)

    scaled, norm_wide = pl.pallas_call(
        prepare_kernel,
        out_shape=[block_shape, jax.ShapeDtypeStruct((row_count, feat_width), F32)],
        in_specs=[HBM] * 2,
        out_specs=[VMEM] * 2,
        scratch_shapes=[
            pltpu.VMEM((row_tiles, tile), jnp.int32),
            pltpu.VMEM((row_count, feat_width), BF),
            pltpu.SemaphoreType.DMA((2,)),
        ],
        compiler_params=params(16),
        cost_estimate=SMALL,
        name="prepare",
    )(in_hbm(degrees.reshape(row_tiles, tile)), in_hbm(features))

    source = {place: move(scaled, rep_partner(place)) for place in far_first(rep_count)}
    source = [scaled] + [source[place] for place in range(1, rep_count)]

    def stage(earlier):
        return pl.pallas_call(
            stage_kernel,
            out_shape=jax.ShapeDtypeStruct((slot_total, tile, tile), BF),
            in_specs=[HBM, ANY],
            out_specs=VMEM,
            scratch_shapes=[pltpu.SemaphoreType.DMA],
            compiler_params=params(16),
            cost_estimate=cost(0, 2 * slot_total * tile * tile * 2),
            name="stage_tiles",
        )(in_hbm(tile_weights[0, 0]), earlier)

    tiles_dev = stage(scaled)

    def forward(places, unrolls, earlier):
        single = 3 in places
        pairs = len(places) - single
        shape = jax.ShapeDtypeStruct((pairs * row_count, feat_width), BF)
        return pl.pallas_call(
            functools.partial(forward_kernel, places, unrolls),
            out_shape=[shape, shape] + [block_shape] * single,
            in_specs=[ANY, SMEM, SMEM, SMEM] + [VMEM] * (1 + rep_count),
            out_specs=[VMEM] * (2 + single),
            scratch_shapes=[
                pltpu.VMEM((col_tiles * tile, feat_width), BF),
                pltpu.VMEM((((2 * pairs + single) * row_tiles + 1) * tile, feat_width), F32),
            ],
            compiler_params=params(16),
            cost_estimate=SMALL,
            name="forward_" + "_".join(map(str, places)),
        )(earlier, bounds, row_place, col_place, tiles_dev, *source)

    def add(a, b):
        return (a.astype(F32) + b.astype(F32)).astype(BF)

    keep, send, part3 = forward((1, 2, 3), (16, 16, 12), norm_wide)
    sums = add(keep, swap_cores(send))
    came3 = move(part3, pair_partner(3, False))
    came2 = move(sums[row_count:], pair_partner(2, False))
    came1 = move(sums[:row_count], pair_partner(1, False))
    keep0, send0 = forward((0,), (16,), send)
    cross0 = swap_cores(send0)

    hidden, scaled_grad, aggregated, pre_grad = pl.pallas_call(
        dense_kernel,
        out_shape=[
            jax.ShapeDtypeStruct((row_count, hid_width), BF),
            block_shape,
            block_shape,
            jax.ShapeDtypeStruct((row_count, hid_width), BF),
        ],
        in_specs=[VMEM] * 10,
        out_specs=[VMEM] * 4,
        compiler_params=params(16),
        cost_estimate=SMALL,
        name="dense",
    )(keep0, cross0, came1, came2, came3, scaled, norm_wide, weight, layer_bias[None], upstream)

    grads2 = move(scaled_grad, pair_partner(2, True))
    grads3 = move(scaled_grad, pair_partner(3, True))
    grads1 = move(scaled_grad, pair_partner(1, True))

    total_shape = jax.ShapeDtypeStruct(((col_tiles + 1) * tile, feat_width), F32)

    tiles_hbm = in_hbm(tile_weights[0, 0])

    def backward(places, unroll, old, blocks):
        last = len(places) > 1
        out_shape = [total_shape]
        if last:
            out_shape = [jax.ShapeDtypeStruct((row_count, feat_width), F32)] + [block_shape] * (rep_count - 1)
        fetches = slot_total // unroll + len(places)
        return pl.pallas_call(
            functools.partial(backward_kernel, places, unroll, old is None, last),
            out_shape=out_shape,
            in_specs=[SMEM, SMEM, SMEM, HBM] + [VMEM] * ((old is not None) + len(blocks)),
            out_specs=[VMEM] * len(out_shape),
            scratch_shapes=[
                pltpu.VMEM(total_shape.shape, F32),
                pltpu.VMEM((sum(part.shape[0] for part in blocks), feat_width), BF),
                pltpu.VMEM((fetches, unroll, tile, tile), BF),
                pltpu.SemaphoreType.DMA((fetches,)),
            ],
            compiler_params=params(28),
            cost_estimate=SMALL,
            name="backward_" + "_".join(map(str, places)),
        )(bounds, row_place, col_place, tiles_hbm, *([] if old is None else [old]), *blocks)

    grad_rows = feat_width // CORES
    half_shape = jax.ShapeDtypeStruct((grad_rows + BIAS_ROWS, hid_width), F32)

    (total,) = backward((0,), 16, None, [scaled_grad, swap_cores(scaled_grad)])
    halves = pl.pallas_call(
        weight_kernel,
        out_shape=[half_shape] * 2,
        in_specs=[SMEM, VMEM, VMEM, ANY],
        out_specs=[VMEM] * 2,
        scratch_shapes=[pltpu.VMEM((feat_width, hid_width), F32)],
        compiler_params=params(16),
        cost_estimate=SMALL,
        name="weight_terms",
    )(core[None].astype(jnp.int32), aggregated, pre_grad, total)

    def rep_sum(keep, send):
        grad = keep + swap_cores(send)
        for n in range(rep_bits()):
            grad = grad + move(grad.astype(BF), rep_partner(1 << n)).astype(F32)
        return grad

    grad = block(rep_sum, *halves)
    blk_bits = (blk_count - 1).bit_length()
    grads1, grads2, grads3 = together([grads1, grads2, grads3], [grad])
    near_far = jnp.concatenate([grads1, grads2])
    other = swap_cores(near_far)
    (total,) = backward((3,), 10, total, [grads3])
    came = move(grad.astype(BF), lambda r, k: (r, k ^ 2))
    (total,) = together([total], [came])
    columns = backward((1, 2), 16, total, [near_far, other])

    def finish_weight(grad, came):
        grad = grad + came.astype(F32)
        for bit in range(2, blk_bits):
            grad = grad + move(grad.astype(BF), lambda r, k: (r, k ^ (1 << bit))).astype(F32)
        grad = grad * (row_count * rep_count * blk_count) ** (-0.5)
        mine = grad[:grad_rows]
        other = swap_cores(mine)
        weight_grad = jnp.where(
            core == 0, jnp.concatenate([mine, other]), jnp.concatenate([other, mine])
        )
        return weight_grad, grad[grad_rows]

    column_sum = columns[0]
    arrived = {place: move(columns[place], rep_partner(place)) for place in far_first(rep_count)}
    weight_grad, bias_grad = block(finish_weight, grad, came)
    for place in range(1, rep_count):
        column_sum = column_sum + arrived[place].astype(F32)
    feature_grad = (norm_wide * (column_sum + scaled_grad.astype(F32))).astype(BF)
    return (hidden, feature_grad, weight_grad, bias_grad)


def solution(mesh):
    placed = (
        P(("rep", "blk"), None),
        P(("rep", "blk")),
        P("rep", "blk", None, None, None),
        P("rep", "blk", None),
        P("rep", "blk", None),
        P("rep", "blk"),
        P(),
        P(),
        P(("rep", "blk"), None),
    )
    return jax.shard_map(
        on_device,
        mesh=mesh,
        in_specs=placed,
        out_specs=(P(("rep", "blk"), None), P(("rep", "blk"), None), P(), P()),
        check_vma=False,
    )
```

```python
import functools

import jax
import jax.numpy as jnp
from jax import lax
from jax.experimental import pallas as pl
from jax.experimental.pallas import tpu as pltpu
from jax.sharding import PartitionSpec as P

BOTH = ("rep", "blk")
VMEM = pl.BlockSpec(memory_space=pltpu.VMEM)
SMEM = pl.BlockSpec(memory_space=pltpu.SMEM)
ANY = pl.BlockSpec(memory_space=pl.ANY)
HBM = pl.BlockSpec(memory_space=pltpu.HBM)
BF = jnp.bfloat16
F32 = jnp.float32
CORES = 2
BIAS_ROWS = 16


def params(mib):
    return pltpu.CompilerParams(vmem_limit_bytes=mib * 1024 * 1024)


def cost(flops, size):
    return pl.CostEstimate(flops=flops, bytes_accessed=size, transcendentals=0)


SMALL = cost(0, 1024)
LARGE = cost(0, 2**26)


def node_scale(degrees):
    return 1.0 / jnp.sqrt(degrees.astype(F32) + 1.0)


def in_hbm(value):
    return pltpu.with_memory_space_constraint(value, pltpu.HBM)


def move(value, target):
    rep_count, blk_count = lax.axis_size("rep"), lax.axis_size("blk")
    pairs = []
    for r in range(rep_count):
        for k in range(blk_count):
            to_r, to_k = target(r, k)
            pairs.append((r * blk_count + k, to_r * blk_count + to_k))
    return lax.ppermute(value, BOTH, pairs)


def block(function, *args):
    shapes = jax.eval_shape(function, *args)
    return lax.cond(
        lax.axis_index("blk") < lax.axis_size("blk"),
        function,
        lambda *unused: jax.tree.map(lambda shape: jnp.zeros(shape.shape, shape.dtype), shapes),
        *args,
    )


def swap_cores(value):
    return move(value, lambda r, k: (r, k ^ 1))


def rep_bits():
    return (lax.axis_size("rep") - 1).bit_length()


def rep_partner(place):
    bits = rep_bits()
    turned = sum(((place >> n) & 1) << ((n + 1) % bits) for n in range(bits))
    return lambda r, k: (r ^ (turned if k % 2 else place), k)


def rep_place(rep_ids, rep_index, core):
    bits = rep_bits()
    relative = rep_ids ^ rep_index
    place = jnp.zeros_like(relative)
    for n in range(bits):
        turned = (relative >> ((n + 1) % bits)) & 1
        place = place + (jnp.where(core == 0, (relative >> n) & 1, turned) << n)
    return place


def far_first(count):
    return sorted(range(1, count), key=lambda place: -bin(place).count("1"))


def pair_at(place, pair_index, core):
    pairs = lax.axis_size("blk") // CORES
    if pairs == 4:
        return pair_index ^ (0, 1, 3, 2)[place]
    step = (0, 1, -1, jnp.where(core == 0, -2, 2))[place]
    return (pair_index + step) % pairs


def pair_partner(place, back, other_core=False):
    blk_count = lax.axis_size("blk")
    if other_core:
        near = pair_partner(place, back)
        return lambda r, k: (r, near(r, k)[1] ^ 1)

    def target(r, k):
        if place == 3:
            return (r, (k + (3 if k % 2 else -3)) % blk_count)
        if blk_count == 8:
            return (r, k ^ {1: 2, 2: 6}[place])
        step = {1: 2, 2: -2}[place]
        return (r, (k + (-step if back else step)) % blk_count)

    return target


def together(values, earlier=(), weigh=None):
    count = len(values)
    return pl.pallas_call(
        lambda *refs: None,
        out_shape=[jax.ShapeDtypeStruct(value.shape, value.dtype) for value in values],
        in_specs=[ANY] * (count + len(earlier)),
        out_specs=[ANY] * count,
        input_output_aliases={n: n for n in range(count)},
        compiler_params=params(16),
        cost_estimate=weigh or SMALL,
        name="together",
    )(*values, *earlier)


def prepare_kernel(degrees_hbm, features_hbm, scaled_ref, norm_ref, degrees_ref, features_ref, sems):
    copies = [
        pltpu.make_async_copy(degrees_hbm, degrees_ref, sems.at[0]),
        pltpu.make_async_copy(features_hbm, features_ref, sems.at[1]),
    ]
    for copy in copies:
        copy.start()
    for copy in copies:
        copy.wait()
    tile = degrees_ref.shape[1]
    for n in range(degrees_ref.shape[0]):
        norm = node_scale(degrees_ref[n : n + 1, :])
        norm = jnp.broadcast_to(norm, (tile, tile)).T
        rows = slice(n * tile, (n + 1) * tile)
        norm_ref[rows, :] = norm
        scaled_ref[rows, :] = (norm * features_ref[rows, :].astype(F32)).astype(BF)


def stage_kernel(w_ref, earlier_ref, out_ref, sem):
    copy = pltpu.make_async_copy(w_ref, out_ref, sem)
    copy.start()
    copy.wait()


def gather_blocks(block_refs, held):
    first = 0
    for block_ref in block_refs:
        held[first : first + block_ref.shape[0], :] = block_ref[...]
        first += block_ref.shape[0]


def over_slots(low, high, unroll, slot_total, body):
    def step(i, carry):
        for u in range(unroll):
            t = low + i * unroll + u
            body(jnp.minimum(t, slot_total - 1), t < high)
        return carry

    lax.fori_loop(0, (high - low + unroll - 1) // unroll, step, 0)


def aligned(index, tile):
    return pl.ds(pl.multiple_of(index * tile, tile), tile)


def forward_kernel(places, unrolls, earlier_ref, bounds_ref, row_ref, col_ref, w_ref, *refs):
    outs = 3 if 3 in places else 2
    x_refs, out_refs, (held, total) = refs[: -2 - outs], refs[-2 - outs : -2], refs[-2:]
    tile = w_ref.shape[-1]
    block_tiles = x_refs[0].shape[0] // tile
    gather_blocks(x_refs, held)
    total[...] = jnp.zeros_like(total)
    spare = total.shape[0] // tile - 1
    for n, place in enumerate(places):

        def body(t, used):
            row = row_ref[t]
            if place == 3:
                row = row % block_tiles
            row = jnp.where(used, row + n * 2 * block_tiles, spare)
            part = jnp.dot(w_ref[t], held[aligned(col_ref[t], tile), :], preferred_element_type=F32)
            total[aligned(row, tile), :] += part

        over_slots(bounds_ref[place], bounds_ref[4 + place], unrolls[n], w_ref.shape[0], body)
    rows = block_tiles * tile
    for n, place in enumerate(places):
        first = n * 2 * rows
        if place == 3:
            out_refs[2][...] = total[first : first + rows, :].astype(BF)
        else:
            for out_ref in out_refs[:2]:
                out_ref[n * rows : (n + 1) * rows, :] = total[first : first + rows, :].astype(BF)
                first += rows


def stream_slots(w_hbm, held, sems, ranges, unroll):
    slot_total = w_hbm.shape[0]
    begins = [0]
    for low, high in ranges:
        begins.append(begins[-1] + (high - low + unroll - 1) // unroll)

    def fetch(low, i, place):
        first = jnp.minimum(low + i * unroll, slot_total - unroll)
        return first, pltpu.make_async_copy(w_hbm.at[pl.ds(first, unroll)], held.at[place], sems.at[place])

    for n, (low, high) in enumerate(ranges):

        def start(i, carry, low=low, begin=begins[n]):
            fetch(low, i, begin + i)[1].start()
            return carry

        lax.fori_loop(0, begins[n + 1] - begins[n], start, 0)

    def finish(body):
        for n, (low, high) in enumerate(ranges):

            def step(i, carry, low=low, high=high, n=n, begin=begins[n]):
                first, copy = fetch(low, i, begin + i)
                copy.wait()
                for u in range(unroll):
                    t = first + u
                    body(held[begin + i, u], t, (t >= low + i * unroll) & (t < high), n)
                return carry

            lax.fori_loop(0, begins[n + 1] - begins[n], step, 0)

    return finish


def backward_kernel(places, unroll, bounds_ref, row_ref, col_ref, w_ref, *refs):
    refs, (total, held, tiles_held, sems) = refs[:-4], refs[-4:]
    ranges = [(bounds_ref[place], bounds_ref[4 + place]) for place in places]
    finish = stream_slots(w_ref, tiles_held, sems, ranges, unroll)
    tile = w_ref.shape[-1]
    block_refs, out_refs = (refs[:2], refs[2:]) if places == (0,) else (refs[1:4], refs[4:])
    if places == (0,):
        total[...] = jnp.zeros_like(total)
    else:
        used_rows = refs[0].shape[0]
        total[:used_rows, :] = refs[0][...].astype(F32)
        total[used_rows:, :] = jnp.zeros((total.shape[0] - used_rows, total.shape[1]), F32)
    gather_blocks(block_refs, held)
    spare = total.shape[0] // tile - 1
    block_tiles = held.shape[0] // tile // (2 if places == (0,) else 5)

    def body(w, t, used, n):
        row = row_ref[t]
        if places[n] == 3:
            row = row % block_tiles + 4 * block_tiles
        elif places[n] > 0:
            row = jnp.where(row < block_tiles, row, row + block_tiles) + n * block_tiles
        part = lax.dot_general(
            w, held[aligned(row, tile), :], (((0,), (0,)), ((), ())), preferred_element_type=F32
        )
        total[aligned(jnp.where(used, col_ref[t], spare), tile), :] += part

    finish(body)
    first = 0
    for out_ref in out_refs:
        rows = out_ref.shape[0]
        out_ref[...] = total[first : first + rows, :].astype(out_ref.dtype)
        first += rows


def dense_kernel(*refs):
    part_refs, (norm_ref, weight_ref, bias_ref, up_ref) = refs[:-8], refs[-8:-4]
    hidden_ref, grad_ref, aggregated_ref, pre_grad_ref = refs[-4:]
    norm = norm_ref[...]
    neighbor = part_refs[0][...].astype(F32)
    for part_ref in part_refs[1:]:
        neighbor = neighbor + part_ref[...].astype(F32)
    aggregated = (norm * neighbor).astype(BF)
    weight = weight_ref[...]
    pre_act = jnp.dot(aggregated, weight, preferred_element_type=F32) + bias_ref[...]
    gate = 1.0 / (1.0 + jnp.exp(-pre_act))
    hidden_ref[...] = (pre_act * gate).astype(BF)
    pre_grad = (up_ref[...].astype(F32) * (gate + pre_act * gate * (1.0 - gate))).astype(BF)
    back = lax.dot_general(pre_grad, weight, (((1,), (1,)), ((), ())), preferred_element_type=F32)
    grad_ref[...] = (norm * back).astype(BF)
    aggregated_ref[...] = aggregated
    pre_grad_ref[...] = pre_grad


def weight_kernel(core_ref, aggregated_ref, pre_grad_ref, keep_ref, send_ref, full):
    pre_grad = pre_grad_ref[...]
    half = full.shape[0] // CORES
    full[...] = lax.dot_general(
        aggregated_ref[...], pre_grad, (((0,), (0,)), ((), ())), preferred_element_type=F32
    )
    sums = jnp.sum(pre_grad.astype(F32), axis=0, keepdims=True)
    sums = jnp.broadcast_to(sums, (BIAS_ROWS, pre_grad.shape[1]))
    core = core_ref[0]
    for out_ref, side in ((keep_ref, core), (send_ref, 1 - core)):
        out_ref[:half, :] = full[aligned(side, half), :]
        out_ref[half:, :] = sums


def on_device(
    features, degrees, tile_weights, tile_rows, tile_cols, tile_counts, weight, layer_bias, upstream
):
    row_count, feat_width = features.shape
    hid_width = weight.shape[1]
    slot_total, tile = tile_weights.shape[2], tile_weights.shape[-1]
    row_tiles = row_count // tile
    rep_count, blk_count = lax.axis_size("rep"), lax.axis_size("blk")
    rep_index, blk_index = lax.axis_index("rep"), lax.axis_index("blk")
    core, pair_index = blk_index % CORES, blk_index // CORES
    col_tiles = rep_count * row_tiles
    block_shape = jax.ShapeDtypeStruct((row_count, feat_width), BF)

    rows_dev, cols_dev, count_dev = tile_rows[0, 0], tile_cols[0, 0], tile_counts[0, 0]
    used = jnp.arange(slot_total, dtype=jnp.int32) < count_dev
    group = rows_dev // row_tiles
    row_place = jnp.where(group % CORES == core, 0, row_tiles) + rows_dev % row_tiles
    col_place = rep_place(cols_dev // row_tiles, rep_index, core) * row_tiles + cols_dev % row_tiles
    pair_ids = jnp.stack([pair_at(place, pair_index, core) for place in range(4)])
    pair_ids = jnp.concatenate([pair_ids, pair_ids + 1])
    bounds = jnp.sum(used & (group // CORES < pair_ids[:, None]), axis=1).astype(jnp.int32)
    row_place, col_place = row_place.astype(jnp.int32), col_place.astype(jnp.int32)

    scaled, norm_wide = pl.pallas_call(
        prepare_kernel,
        out_shape=[block_shape, jax.ShapeDtypeStruct((row_count, feat_width), F32)],
        in_specs=[HBM] * 2,
        out_specs=[VMEM] * 2,
        scratch_shapes=[
            pltpu.VMEM((row_tiles, tile), jnp.int32),
            pltpu.VMEM((row_count, feat_width), BF),
            pltpu.SemaphoreType.DMA((2,)),
        ],
        compiler_params=params(16),
        cost_estimate=SMALL,
        name="prepare",
    )(in_hbm(degrees.reshape(row_tiles, tile)), in_hbm(features))

    source = {place: move(scaled, rep_partner(place)) for place in far_first(rep_count)}
    source = [scaled] + [source[place] for place in range(1, rep_count)]

    def stage(earlier):
        return pl.pallas_call(
            stage_kernel,
            out_shape=jax.ShapeDtypeStruct((slot_total, tile, tile), BF),
            in_specs=[HBM, ANY],
            out_specs=VMEM,
            scratch_shapes=[pltpu.SemaphoreType.DMA],
            compiler_params=params(16),
            cost_estimate=cost(0, 2 * slot_total * tile * tile * 2),
            name="stage_tiles",
        )(in_hbm(tile_weights[0, 0]), earlier)

    tiles_dev = stage(scaled)

    def forward(places, unrolls, earlier):
        single = 3 in places
        pairs = len(places) - single
        shape = jax.ShapeDtypeStruct((pairs * row_count, feat_width), BF)
        return pl.pallas_call(
            functools.partial(forward_kernel, places, unrolls),
            out_shape=[shape, shape] + [block_shape] * single,
            in_specs=[ANY, SMEM, SMEM, SMEM] + [VMEM] * (1 + rep_count),
            out_specs=[VMEM] * (2 + single),
            scratch_shapes=[
                pltpu.VMEM((col_tiles * tile, feat_width), BF),
                pltpu.VMEM((((2 * pairs + single) * row_tiles + 1) * tile, feat_width), F32),
            ],
            compiler_params=params(16),
            cost_estimate=SMALL,
            name="forward_" + "_".join(map(str, places)),
        )(earlier, bounds, row_place, col_place, tiles_dev, *source)

    def add(a, b):
        return (a.astype(F32) + b.astype(F32)).astype(BF)

    keep, send, part3 = forward((1, 2, 3), (16, 16, 12), norm_wide)
    sums = add(keep, swap_cores(send))
    came3 = move(part3, pair_partner(3, False))
    came2 = move(sums[row_count:], pair_partner(2, False))
    came1 = move(sums[:row_count], pair_partner(1, False))
    keep0, send0 = forward((0,), (16,), send)
    cross0 = swap_cores(send0)

    hidden, scaled_grad, aggregated, pre_grad = pl.pallas_call(
        dense_kernel,
        out_shape=[
            jax.ShapeDtypeStruct((row_count, hid_width), BF),
            block_shape,
            block_shape,
            jax.ShapeDtypeStruct((row_count, hid_width), BF),
        ],
        in_specs=[VMEM] * 10,
        out_specs=[VMEM] * 4,
        compiler_params=params(16),
        cost_estimate=SMALL,
        name="dense",
    )(keep0, cross0, came1, came2, came3, scaled, norm_wide, weight, layer_bias[None], upstream)

    grads2 = move(scaled_grad, pair_partner(2, True))
    grads3 = move(scaled_grad, pair_partner(3, True))
    grads1 = move(scaled_grad, pair_partner(1, True))

    tiles_hbm = in_hbm(tile_weights[0, 0])
    column_shape = jax.ShapeDtypeStruct((col_tiles * tile, feat_width), BF)

    def backward(places, unroll, out_shape, *blocks):
        fetches = slot_total // unroll + len(places)
        held_rows = (2 if places == (0,) else 5) * row_count
        return pl.pallas_call(
            functools.partial(backward_kernel, places, unroll),
            out_shape=out_shape,
            in_specs=[SMEM, SMEM, SMEM, HBM] + [VMEM] * len(blocks),
            out_specs=[VMEM] * len(out_shape),
            scratch_shapes=[
                pltpu.VMEM(((col_tiles + 1) * tile, feat_width), F32),
                pltpu.VMEM((held_rows, feat_width), BF),
                pltpu.VMEM((fetches, unroll, tile, tile), BF),
                pltpu.SemaphoreType.DMA((fetches,)),
            ],
            compiler_params=params(28),
            cost_estimate=SMALL,
            name="backward_" + "_".join(map(str, places)),
        )(bounds, row_place, col_place, tiles_hbm, *blocks)

    grad_rows = feat_width // CORES
    half_shape = jax.ShapeDtypeStruct((grad_rows + BIAS_ROWS, hid_width), F32)

    def own_pair(scaled_grad, aggregated, pre_grad):
        other = swap_cores(scaled_grad)
        keep, send = pl.pallas_call(
            weight_kernel,
            out_shape=[half_shape] * 2,
            in_specs=[SMEM, VMEM, VMEM],
            out_specs=[VMEM] * 2,
            scratch_shapes=[pltpu.VMEM((feat_width, hid_width), F32)],
            compiler_params=params(16),
            cost_estimate=SMALL,
            name="weight_terms",
        )(core[None].astype(jnp.int32), aggregated, pre_grad)
        grad = keep + swap_cores(send)
        (total,) = backward((0,), 16, [column_shape], scaled_grad, other)
        for n in range(rep_bits()):
            came = move(grad.astype(BF), rep_partner(1 << n))
            if n == 0:
                (grad,) = together([grad], [total])
            grad = grad + came.astype(F32)
        return total, grad

    total, grad = block(own_pair, scaled_grad, aggregated, pre_grad)
    blk_bits = (blk_count - 1).bit_length()
    grads1, grads2, grads3 = together([grads1, grads2, grads3], [grad])
    near_far = jnp.concatenate([grads1, grads2])
    came = move(grad.astype(BF), lambda r, k: (r, k ^ 2))
    column_shapes = [jax.ShapeDtypeStruct((row_count, feat_width), F32)] + [block_shape] * (rep_count - 1)
    columns = backward((1, 2, 3), 16, column_shapes, total, near_far, swap_cores(near_far), grads3)
    columns = together(columns, [came])

    def finish_weight(grad, came):
        grad = grad + came.astype(F32)
        for bit in range(2, blk_bits):
            grad = grad + move(grad.astype(BF), lambda r, k: (r, k ^ (1 << bit))).astype(F32)
        grad = grad * (row_count * rep_count * blk_count) ** (-0.5)
        mine = grad[:grad_rows]
        other = swap_cores(mine)
        weight_grad = jnp.where(
            core == 0, jnp.concatenate([mine, other]), jnp.concatenate([other, mine])
        )
        return weight_grad, grad[grad_rows]

    column_sum = columns[0]
    arrived = {place: move(columns[place], rep_partner(place)) for place in far_first(rep_count)}
    weight_grad, bias_grad = block(finish_weight, grad, came)
    for place in range(1, rep_count):
        column_sum = column_sum + arrived[place].astype(F32)
    feature_grad = (norm_wide * (column_sum + scaled_grad.astype(F32))).astype(BF)
    return (hidden, feature_grad, weight_grad, bias_grad)


def solution(mesh):
    placed = (
        P(("rep", "blk"), None),
        P(("rep", "blk")),
        P("rep", "blk", None, None, None),
        P("rep", "blk", None),
        P("rep", "blk", None),
        P("rep", "blk"),
        P(),
        P(),
        P(("rep", "blk"), None),
    )
    return jax.shard_map(
        on_device,
        mesh=mesh,
        in_specs=placed,
        out_specs=(P(("rep", "blk"), None), P(("rep", "blk"), None), P(), P()),
        check_vma=False,
    )
```

```python
import functools

import jax
import jax.numpy as jnp
from jax import lax
from jax.experimental import pallas as pl
from jax.experimental.pallas import tpu as pltpu
from jax.sharding import PartitionSpec as P

BOTH = ("rep", "blk")
VMEM = pl.BlockSpec(memory_space=pltpu.VMEM)
SMEM = pl.BlockSpec(memory_space=pltpu.SMEM)
ANY = pl.BlockSpec(memory_space=pl.ANY)
HBM = pl.BlockSpec(memory_space=pltpu.HBM)
BF = jnp.bfloat16
F32 = jnp.float32
CORES = 2
BIAS_ROWS = 16


def params(mib):
    return pltpu.CompilerParams(vmem_limit_bytes=mib * 1024 * 1024)


def cost(flops, size):
    return pl.CostEstimate(flops=flops, bytes_accessed=size, transcendentals=0)


SMALL = cost(0, 1024)
LARGE = cost(0, 2**26)


def node_scale(degrees):
    return 1.0 / jnp.sqrt(degrees.astype(F32) + 1.0)


def in_hbm(value):
    return pltpu.with_memory_space_constraint(value, pltpu.HBM)


def move(value, target):
    rep_count, blk_count = lax.axis_size("rep"), lax.axis_size("blk")
    pairs = []
    for r in range(rep_count):
        for k in range(blk_count):
            to_r, to_k = target(r, k)
            pairs.append((r * blk_count + k, to_r * blk_count + to_k))
    return lax.ppermute(value, BOTH, pairs)


def block(function, *args):
    shapes = jax.eval_shape(function, *args)
    return lax.cond(
        lax.axis_index("blk") < lax.axis_size("blk"),
        function,
        lambda *unused: jax.tree.map(lambda shape: jnp.zeros(shape.shape, shape.dtype), shapes),
        *args,
    )


def swap_cores(value):
    return move(value, lambda r, k: (r, k ^ 1))


def rep_bits():
    return (lax.axis_size("rep") - 1).bit_length()


def rep_partner(place):
    bits = rep_bits()
    turned = sum(((place >> n) & 1) << ((n + 1) % bits) for n in range(bits))
    return lambda r, k: (r ^ (turned if k % 2 else place), k)


def rep_place(rep_ids, rep_index, core):
    bits = rep_bits()
    relative = rep_ids ^ rep_index
    place = jnp.zeros_like(relative)
    for n in range(bits):
        turned = (relative >> ((n + 1) % bits)) & 1
        place = place + (jnp.where(core == 0, (relative >> n) & 1, turned) << n)
    return place


def far_first(count):
    return sorted(range(1, count), key=lambda place: -bin(place).count("1"))


def pair_at(place, pair_index, core):
    pairs = lax.axis_size("blk") // CORES
    if pairs == 4:
        return pair_index ^ (0, 1, 3, 2)[place]
    step = (0, 1, -1, jnp.where(core == 0, -2, 2))[place]
    return (pair_index + step) % pairs


def pair_partner(place, back, other_core=False):
    blk_count = lax.axis_size("blk")
    if other_core:
        near = pair_partner(place, back)
        return lambda r, k: (r, near(r, k)[1] ^ 1)

    def target(r, k):
        if place == 3:
            return (r, (k + (3 if k % 2 else -3)) % blk_count)
        if blk_count == 8:
            return (r, k ^ {1: 2, 2: 6}[place])
        step = {1: 2, 2: -2}[place]
        return (r, (k + (-step if back else step)) % blk_count)

    return target


def together(values, earlier=(), weigh=None):
    count = len(values)
    return pl.pallas_call(
        lambda *refs: None,
        out_shape=[jax.ShapeDtypeStruct(value.shape, value.dtype) for value in values],
        in_specs=[ANY] * (count + len(earlier)),
        out_specs=[ANY] * count,
        input_output_aliases={n: n for n in range(count)},
        compiler_params=params(16),
        cost_estimate=weigh or SMALL,
        name="together",
    )(*values, *earlier)


def prepare_kernel(degrees_hbm, features_hbm, scaled_ref, norm_ref, degrees_ref, features_ref, sems):
    copies = [
        pltpu.make_async_copy(degrees_hbm, degrees_ref, sems.at[0]),
        pltpu.make_async_copy(features_hbm, features_ref, sems.at[1]),
    ]
    for copy in copies:
        copy.start()
    for copy in copies:
        copy.wait()
    tile = degrees_ref.shape[1]
    for n in range(degrees_ref.shape[0]):
        norm = node_scale(degrees_ref[n : n + 1, :])
        norm = jnp.broadcast_to(norm, (tile, tile)).T
        rows = slice(n * tile, (n + 1) * tile)
        norm_ref[rows, :] = norm
        scaled_ref[rows, :] = (norm * features_ref[rows, :].astype(F32)).astype(BF)


def write_kernel(value_ref, out_ref, sem):
    copy = pltpu.make_async_copy(value_ref, out_ref, sem)
    copy.start()
    copy.wait()


def stage_kernel(w_ref, earlier_ref, out_ref, sem):
    copy = pltpu.make_async_copy(w_ref, out_ref, sem)
    copy.start()
    copy.wait()


def gather_blocks(block_refs, held):
    first = 0
    for block_ref in block_refs:
        held[first : first + block_ref.shape[0], :] = block_ref[...]
        first += block_ref.shape[0]


def over_slots(low, high, unroll, slot_total, body):
    def step(i, carry):
        for u in range(unroll):
            t = low + i * unroll + u
            body(jnp.minimum(t, slot_total - 1), t < high)
        return carry

    lax.fori_loop(0, (high - low + unroll - 1) // unroll, step, 0)


def aligned(index, tile):
    return pl.ds(pl.multiple_of(index * tile, tile), tile)


def forward_kernel(places, unrolls, earlier_ref, bounds_ref, row_ref, col_ref, w_ref, *refs):
    outs = 3 if 3 in places else 2
    x_refs, out_refs, (held, total) = refs[: -2 - outs], refs[-2 - outs : -2], refs[-2:]
    tile = w_ref.shape[-1]
    block_tiles = x_refs[0].shape[0] // tile
    gather_blocks(x_refs, held)
    total[...] = jnp.zeros_like(total)
    spare = total.shape[0] // tile - 1
    for n, place in enumerate(places):

        def body(t, used):
            row = row_ref[t]
            if place == 3:
                row = row % block_tiles
            row = jnp.where(used, row + n * 2 * block_tiles, spare)
            part = jnp.dot(w_ref[t], held[aligned(col_ref[t], tile), :], preferred_element_type=F32)
            total[aligned(row, tile), :] += part

        over_slots(bounds_ref[place], bounds_ref[4 + place], unrolls[n], w_ref.shape[0], body)
    rows = block_tiles * tile
    for n, place in enumerate(places):
        first = n * 2 * rows
        if place == 3:
            out_refs[2][...] = total[first : first + rows, :].astype(BF)
        else:
            for out_ref in out_refs[:2]:
                out_ref[n * rows : (n + 1) * rows, :] = total[first : first + rows, :].astype(BF)
                first += rows


def stream_slots(w_hbm, held, sems, ranges, unroll):
    slot_total = w_hbm.shape[0]
    begins = [0]
    for low, high in ranges:
        begins.append(begins[-1] + (high - low + unroll - 1) // unroll)

    def fetch(low, i, place):
        first = jnp.minimum(low + i * unroll, slot_total - unroll)
        return first, pltpu.make_async_copy(w_hbm.at[pl.ds(first, unroll)], held.at[place], sems.at[place])

    for n, (low, high) in enumerate(ranges):

        def start(i, carry, low=low, begin=begins[n]):
            fetch(low, i, begin + i)[1].start()
            return carry

        lax.fori_loop(0, begins[n + 1] - begins[n], start, 0)

    def finish(body):
        for n, (low, high) in enumerate(ranges):

            def step(i, carry, low=low, high=high, n=n, begin=begins[n]):
                first, copy = fetch(low, i, begin + i)
                copy.wait()
                for u in range(unroll):
                    t = first + u
                    body(held[begin + i, u], t, (t >= low + i * unroll) & (t < high), n)
                return carry

            lax.fori_loop(0, begins[n + 1] - begins[n], step, 0)

    return finish


def backward_kernel(places, unroll, bounds_ref, row_ref, col_ref, w_ref, *refs):
    refs, (total, held, tiles_held, sems) = refs[:-4], refs[-4:]
    ranges = [(bounds_ref[place], bounds_ref[4 + place]) for place in places]
    finish = stream_slots(w_ref, tiles_held, sems, ranges, unroll)
    tile = w_ref.shape[-1]
    block_refs, refs = refs[: 2 if places == (0,) else 3], refs[2 if places == (0,) else 3 :]
    if places == (0,):
        out_refs = refs
        total[...] = jnp.zeros_like(total)
    else:
        old_refs, out_refs = refs[: len(refs) // 2], refs[len(refs) // 2 :]
        first = 0
        for old_ref in old_refs:
            total[first : first + old_ref.shape[0], :] = old_ref[...].astype(F32)
            first += old_ref.shape[0]
        total[first:, :] = jnp.zeros((total.shape[0] - first, total.shape[1]), F32)
    gather_blocks(block_refs, held)
    spare = total.shape[0] // tile - 1
    block_tiles = held.shape[0] // tile // (2 if places == (0,) else 5)

    def body(w, t, used, n):
        row = row_ref[t]
        if places[n] == 3:
            row = row % block_tiles + 4 * block_tiles
        elif places[n] > 0:
            row = jnp.where(row < block_tiles, row, row + block_tiles) + n * block_tiles
        part = lax.dot_general(
            w, held[aligned(row, tile), :], (((0,), (0,)), ((), ())), preferred_element_type=F32
        )
        total[aligned(jnp.where(used, col_ref[t], spare), tile), :] += part

    finish(body)
    first = 0
    for out_ref in out_refs:
        rows = out_ref.shape[0]
        out_ref[...] = total[first : first + rows, :].astype(out_ref.dtype)
        first += rows


def dense_kernel(*refs):
    part_refs, (norm_ref, weight_ref, bias_ref, up_ref) = refs[:-8], refs[-8:-4]
    hidden_ref, grad_ref, aggregated_ref, pre_grad_ref = refs[-4:]
    norm = norm_ref[...]
    neighbor = part_refs[0][...].astype(F32)
    for part_ref in part_refs[1:]:
        neighbor = neighbor + part_ref[...].astype(F32)
    aggregated = (norm * neighbor).astype(BF)
    weight = weight_ref[...]
    pre_act = jnp.dot(aggregated, weight, preferred_element_type=F32) + bias_ref[...]
    gate = 0.5 * jnp.tanh(0.5 * pre_act) + 0.5
    hidden_ref[...] = (pre_act * gate).astype(BF)
    pre_grad = (up_ref[...].astype(F32) * (gate + pre_act * gate * (1.0 - gate))).astype(BF)
    back = lax.dot_general(pre_grad, weight, (((1,), (1,)), ((), ())), preferred_element_type=F32)
    grad_ref[...] = (norm * back).astype(BF)
    aggregated_ref[...] = aggregated
    pre_grad_ref[...] = pre_grad


def weight_kernel(core_ref, aggregated_ref, pre_grad_ref, keep_ref, send_ref, full):
    pre_grad = pre_grad_ref[...]
    half = full.shape[0] // CORES
    full[...] = lax.dot_general(
        aggregated_ref[...], pre_grad, (((0,), (0,)), ((), ())), preferred_element_type=F32
    )
    sums = jnp.sum(pre_grad.astype(F32), axis=0, keepdims=True)
    sums = jnp.broadcast_to(sums, (BIAS_ROWS, pre_grad.shape[1]))
    core = core_ref[0]
    for out_ref, side in ((keep_ref, core), (send_ref, 1 - core)):
        out_ref[:half, :] = full[aligned(side, half), :]
        out_ref[half:, :] = sums


def on_device(
    features, degrees, tile_weights, tile_rows, tile_cols, tile_counts, weight, layer_bias, upstream
):
    row_count, feat_width = features.shape
    hid_width = weight.shape[1]
    slot_total, tile = tile_weights.shape[2], tile_weights.shape[-1]
    row_tiles = row_count // tile
    rep_count, blk_count = lax.axis_size("rep"), lax.axis_size("blk")
    rep_index, blk_index = lax.axis_index("rep"), lax.axis_index("blk")
    core, pair_index = blk_index % CORES, blk_index // CORES
    col_tiles = rep_count * row_tiles
    block_shape = jax.ShapeDtypeStruct((row_count, feat_width), BF)

    rows_dev, cols_dev, count_dev = tile_rows[0, 0], tile_cols[0, 0], tile_counts[0, 0]
    used = jnp.arange(slot_total, dtype=jnp.int32) < count_dev
    group = rows_dev // row_tiles
    row_place = jnp.where(group % CORES == core, 0, row_tiles) + rows_dev % row_tiles
    col_place = rep_place(cols_dev // row_tiles, rep_index, core) * row_tiles + cols_dev % row_tiles
    pair_ids = jnp.stack([pair_at(place, pair_index, core) for place in range(4)])
    pair_ids = jnp.concatenate([pair_ids, pair_ids + 1])
    bounds = jnp.sum(used & (group // CORES < pair_ids[:, None]), axis=1).astype(jnp.int32)
    row_place, col_place = row_place.astype(jnp.int32), col_place.astype(jnp.int32)

    scaled, norm_wide = pl.pallas_call(
        prepare_kernel,
        out_shape=[block_shape, jax.ShapeDtypeStruct((row_count, feat_width), F32)],
        in_specs=[HBM] * 2,
        out_specs=[VMEM] * 2,
        scratch_shapes=[
            pltpu.VMEM((row_tiles, tile), jnp.int32),
            pltpu.VMEM((row_count, feat_width), BF),
            pltpu.SemaphoreType.DMA((2,)),
        ],
        compiler_params=params(16),
        cost_estimate=SMALL,
        name="prepare",
    )(in_hbm(degrees.reshape(row_tiles, tile)), in_hbm(features))

    source = {place: move(scaled, rep_partner(place)) for place in far_first(rep_count)}
    source = [scaled] + [source[place] for place in range(1, rep_count)]

    def stage(earlier):
        return pl.pallas_call(
            stage_kernel,
            out_shape=jax.ShapeDtypeStruct((slot_total, tile, tile), BF),
            in_specs=[HBM, ANY],
            out_specs=VMEM,
            scratch_shapes=[pltpu.SemaphoreType.DMA],
            compiler_params=params(16),
            cost_estimate=cost(0, 2 * slot_total * tile * tile * 2),
            name="stage_tiles",
        )(in_hbm(tile_weights[0, 0]), earlier)

    tiles_dev = stage(scaled)

    def forward(places, unrolls, earlier):
        single = 3 in places
        pairs = len(places) - single
        shape = jax.ShapeDtypeStruct((pairs * row_count, feat_width), BF)
        return pl.pallas_call(
            functools.partial(forward_kernel, places, unrolls),
            out_shape=[shape, shape] + [block_shape] * single,
            in_specs=[ANY, SMEM, SMEM, SMEM] + [VMEM] * (1 + rep_count),
            out_specs=[VMEM] * (2 + single),
            scratch_shapes=[
                pltpu.VMEM((col_tiles * tile, feat_width), BF),
                pltpu.VMEM((((2 * pairs + single) * row_tiles + 1) * tile, feat_width), F32),
            ],
            compiler_params=params(16),
            cost_estimate=SMALL,
            name="forward_" + "_".join(map(str, places)),
        )(earlier, bounds, row_place, col_place, tiles_dev, *source)

    def add(a, b):
        return (a.astype(F32) + b.astype(F32)).astype(BF)

    keep, send, part3 = forward((1, 2, 3), (26, 26, 12), norm_wide)
    sums = add(keep, swap_cores(send))
    came3 = move(part3, pair_partner(3, False))
    came2 = move(sums[row_count:], pair_partner(2, False))
    came1 = move(sums[:row_count], pair_partner(1, False))
    keep0, send0 = forward((0,), (20,), send)
    cross0 = swap_cores(send0)

    hidden, scaled_grad, aggregated, pre_grad = pl.pallas_call(
        dense_kernel,
        out_shape=[
            pltpu.VMEM((row_count, hid_width), BF),
            block_shape,
            block_shape,
            jax.ShapeDtypeStruct((row_count, hid_width), BF),
        ],
        in_specs=[VMEM] * 10,
        out_specs=[VMEM] * 4,
        compiler_params=params(16),
        cost_estimate=SMALL,
        name="dense",
    )(keep0, cross0, came1, came2, came3, scaled, norm_wide, weight, layer_bias[None], upstream)

    grads2 = move(scaled_grad, pair_partner(2, True))
    grads3 = move(scaled_grad, pair_partner(3, True))
    grads1 = move(scaled_grad, pair_partner(1, True))

    tiles_hbm = in_hbm(tile_weights[0, 0])

    def backward(places, unroll, out_shape, *blocks):
        fetches = slot_total // unroll + len(places)
        held_rows = (2 if places == (0,) else 5) * row_count
        return pl.pallas_call(
            functools.partial(backward_kernel, places, unroll),
            out_shape=out_shape,
            in_specs=[SMEM, SMEM, SMEM, HBM] + [VMEM] * len(blocks),
            out_specs=[VMEM] * len(out_shape),
            scratch_shapes=[
                pltpu.VMEM(((col_tiles + 1) * tile, feat_width), F32),
                pltpu.VMEM((held_rows, feat_width), BF),
                pltpu.VMEM((fetches, unroll, tile, tile), BF),
                pltpu.SemaphoreType.DMA((fetches,)),
            ],
            compiler_params=params(28),
            cost_estimate=SMALL,
            name="backward_" + "_".join(map(str, places)),
        )(bounds, row_place, col_place, tiles_hbm, *blocks)

    grad_rows = feat_width // CORES
    half_shape = jax.ShapeDtypeStruct((grad_rows + BIAS_ROWS, hid_width), F32)

    def own_pair(scaled_grad, aggregated, pre_grad):
        other = swap_cores(scaled_grad)
        keep, send = pl.pallas_call(
            weight_kernel,
            out_shape=[half_shape] * 2,
            in_specs=[SMEM, VMEM, VMEM],
            out_specs=[VMEM] * 2,
            scratch_shapes=[pltpu.VMEM((feat_width, hid_width), F32)],
            compiler_params=params(16),
            cost_estimate=SMALL,
            name="weight_terms",
        )(core[None].astype(jnp.int32), aggregated, pre_grad)
        grad = keep + swap_cores(send)
        total = backward((0,), 16, [block_shape] * rep_count, scaled_grad, other)
        for n in range(rep_bits()):
            came = move(grad.astype(BF), rep_partner(1 << n))
            if n == 0:
                (grad,) = together([grad], total)
            grad = grad + came.astype(F32)
        return total, grad

    total, grad = block(own_pair, scaled_grad, aggregated, pre_grad)
    blk_bits = (blk_count - 1).bit_length()
    grads1, grads2, grads3 = together([grads1, grads2, grads3], [grad])
    near_far = jnp.concatenate([grads1, grads2])
    came = move(grad.astype(BF), lambda r, k: (r, k ^ 2))
    column_shapes = [jax.ShapeDtypeStruct((row_count, feat_width), F32)] + [block_shape] * (rep_count - 1)
    columns = backward((1, 2, 3), 16, column_shapes, near_far, swap_cores(near_far), grads3, *total)
    columns = together(columns, [came])

    def write(value):
        return pl.pallas_call(
            write_kernel,
            out_shape=jax.ShapeDtypeStruct(value.shape, value.dtype),
            in_specs=[VMEM],
            out_specs=HBM,
            scratch_shapes=[pltpu.SemaphoreType.DMA],
            compiler_params=params(16),
            cost_estimate=SMALL,
            name="write_hidden",
        )(value)

    def finish(grad, came, hidden):
        grad = grad + came.astype(F32)
        for bit in range(2, blk_bits):
            grad = grad + move(grad.astype(BF), lambda r, k: (r, k ^ (1 << bit))).astype(F32)
        grad = grad * (row_count * rep_count * blk_count) ** (-0.5)
        mine = grad[:grad_rows]
        other = swap_cores(mine)
        weight_grad = jnp.where(
            core == 0, jnp.concatenate([mine, other]), jnp.concatenate([other, mine])
        )
        return weight_grad, grad[grad_rows], write(hidden)

    column_sum = columns[0]
    arrived = {place: move(columns[place], rep_partner(place)) for place in far_first(rep_count)}
    weight_grad, bias_grad, hidden = block(finish, grad, came, hidden)
    for place in range(1, rep_count):
        column_sum = column_sum + arrived[place].astype(F32)
    feature_grad = (norm_wide * (column_sum + scaled_grad.astype(F32))).astype(BF)
    return (hidden, feature_grad, weight_grad, bias_grad)


def solution(mesh):
    placed = (
        P(("rep", "blk"), None),
        P(("rep", "blk")),
        P("rep", "blk", None, None, None),
        P("rep", "blk", None),
        P("rep", "blk", None),
        P("rep", "blk"),
        P(),
        P(),
        P(("rep", "blk"), None),
    )
    return jax.shard_map(
        on_device,
        mesh=mesh,
        in_specs=placed,
        out_specs=(P(("rep", "blk"), None), P(("rep", "blk"), None), P(), P()),
        check_vma=False,
    )
```

```python
import functools

import jax
import jax.numpy as jnp
from jax import lax
from jax.experimental import pallas as pl
from jax.experimental.pallas import tpu as pltpu
from jax.sharding import PartitionSpec as P

BOTH = ("rep", "blk")
VMEM = pl.BlockSpec(memory_space=pltpu.VMEM)
SMEM = pl.BlockSpec(memory_space=pltpu.SMEM)
ANY = pl.BlockSpec(memory_space=pl.ANY)
HBM = pl.BlockSpec(memory_space=pltpu.HBM)
BF = jnp.bfloat16
F32 = jnp.float32
CORES = 2
BIAS_ROWS = 16
TOKEN_ROWS = 16


def params(mib):
    return pltpu.CompilerParams(vmem_limit_bytes=mib * 1024 * 1024)


def cost(flops, size):
    return pl.CostEstimate(flops=flops, bytes_accessed=size, transcendentals=0)


SMALL = cost(0, 1024)
LARGE = cost(0, 2**26)


def node_scale(degrees):
    return 1.0 / jnp.sqrt(degrees.astype(F32) + 1.0)


def in_hbm(value):
    return pltpu.with_memory_space_constraint(value, pltpu.HBM)


def move(value, target):
    rep_count, blk_count = lax.axis_size("rep"), lax.axis_size("blk")
    pairs = []
    for r in range(rep_count):
        for k in range(blk_count):
            to_r, to_k = target(r, k)
            pairs.append((r * blk_count + k, to_r * blk_count + to_k))
    return lax.ppermute(value, BOTH, pairs)


def block(function, *args):
    shapes = jax.eval_shape(function, *args)
    return lax.cond(
        lax.axis_index("blk") < lax.axis_size("blk"),
        function,
        lambda *unused: jax.tree.map(lambda shape: jnp.zeros(shape.shape, shape.dtype), shapes),
        *args,
    )


def swap_cores(value):
    return move(value, lambda r, k: (r, k ^ 1))


def rep_bits():
    return (lax.axis_size("rep") - 1).bit_length()


def rep_partner(place):
    bits = rep_bits()
    turned = sum(((place >> n) & 1) << ((n + 1) % bits) for n in range(bits))
    return lambda r, k: (r ^ (turned if k % 2 else place), k)


def rep_place(rep_ids, rep_index, core):
    bits = rep_bits()
    relative = rep_ids ^ rep_index
    place = jnp.zeros_like(relative)
    for n in range(bits):
        turned = (relative >> ((n + 1) % bits)) & 1
        place = place + (jnp.where(core == 0, (relative >> n) & 1, turned) << n)
    return place


def far_first(count):
    return sorted(range(1, count), key=lambda place: -bin(place).count("1"))


def pair_at(place, pair_index, core):
    pairs = lax.axis_size("blk") // CORES
    if pairs == 4:
        return pair_index ^ (0, 1, 3, 2)[place]
    step = (0, 1, -1, jnp.where(core == 0, -2, 2))[place]
    return (pair_index + step) % pairs


def pair_partner(place, back, other_core=False):
    blk_count = lax.axis_size("blk")
    if other_core:
        near = pair_partner(place, back)
        return lambda r, k: (r, near(r, k)[1] ^ 1)

    def target(r, k):
        if place == 3:
            return (r, (k + (3 if k % 2 else -3)) % blk_count)
        if blk_count == 8:
            return (r, k ^ {1: 2, 2: 6}[place])
        step = {1: 2, 2: -2}[place]
        return (r, (k + (-step if back else step)) % blk_count)

    return target


def together(values, earlier=(), weigh=None):
    count = len(values)
    return pl.pallas_call(
        lambda *refs: None,
        out_shape=[jax.ShapeDtypeStruct(value.shape, value.dtype) for value in values],
        in_specs=[ANY] * (count + len(earlier)),
        out_specs=[ANY] * count,
        input_output_aliases={n: n for n in range(count)},
        compiler_params=params(16),
        cost_estimate=weigh or SMALL,
        name="together",
    )(*values, *earlier)


def prepare_kernel(degrees_hbm, features_hbm, scaled_ref, norm_ref, degrees_ref, features_ref, sems):
    copies = [
        pltpu.make_async_copy(degrees_hbm, degrees_ref, sems.at[0]),
        pltpu.make_async_copy(features_hbm, features_ref, sems.at[1]),
    ]
    for copy in copies:
        copy.start()
    for copy in copies:
        copy.wait()
    tile = degrees_ref.shape[1]
    for n in range(degrees_ref.shape[0]):
        norm = node_scale(degrees_ref[n : n + 1, :])
        norm = jnp.broadcast_to(norm, (tile, tile)).T
        rows = slice(n * tile, (n + 1) * tile)
        norm_ref[rows, :] = norm
        scaled_ref[rows, :] = (norm * features_ref[rows, :].astype(F32)).astype(BF)


def write_kernel(value_ref, out_ref, sem):
    copy = pltpu.make_async_copy(value_ref, out_ref, sem)
    copy.start()
    copy.wait()


def stage_kernel(w_ref, earlier_ref, out_ref, sem):
    copy = pltpu.make_async_copy(w_ref, out_ref, sem)
    copy.start()
    copy.wait()


def gather_blocks(block_refs, held):
    first = 0
    for block_ref in block_refs:
        held[first : first + block_ref.shape[0], :] = block_ref[...]
        first += block_ref.shape[0]


def aligned(index, tile):
    return pl.ds(pl.multiple_of(index * tile, tile), tile)


def stream_slots(w_hbm, held, sems, ranges, unroll):
    slot_total = w_hbm.shape[0]
    begins = [0]
    for low, high in ranges:
        begins.append(begins[-1] + (high - low + unroll - 1) // unroll)

    def fetch(low, i, place):
        first = jnp.minimum(low + i * unroll, slot_total - unroll)
        return first, pltpu.make_async_copy(w_hbm.at[pl.ds(first, unroll)], held.at[place], sems.at[place])

    for n, (low, high) in enumerate(ranges):

        def start(i, carry, low=low, begin=begins[n]):
            fetch(low, i, begin + i)[1].start()
            return carry

        lax.fori_loop(0, begins[n + 1] - begins[n], start, 0)

    def finish(body):
        for n, (low, high) in enumerate(ranges):

            def step(i, carry, low=low, high=high, n=n, begin=begins[n]):
                first, copy = fetch(low, i, begin + i)
                copy.wait()
                for u in range(unroll):
                    t = first + u
                    body(held[begin + i, u], t, (t >= low + i * unroll) & (t < high), n)
                return carry

            lax.fori_loop(0, begins[n + 1] - begins[n], step, 0)

    return finish


def held_slots(w_ref, ranges, unroll):
    slot_total = w_ref.shape[0]

    def finish(body):
        for n, (low, high) in enumerate(ranges):

            def step(i, carry, low=low, high=high, n=n):
                for u in range(unroll):
                    t = low + i * unroll + u
                    place = jnp.minimum(t, slot_total - 1)
                    body(w_ref[place], place, t < high, n)
                return carry

            lax.fori_loop(0, (high - low + unroll - 1) // unroll, step, 0)

    return finish


def forward_kernel(places, unroll, stream, earlier_ref, bounds_ref, row_ref, col_ref, w_ref, *refs):
    ranges = [(bounds_ref[place], bounds_ref[4 + place]) for place in places]
    if stream:
        refs, (tiles_held, sems) = refs[:-2], refs[-2:]
        finish = stream_slots(w_ref, tiles_held, sems, ranges, unroll)
    else:
        finish = held_slots(w_ref, ranges, unroll)
    outs = 1 if 3 in places else 2
    x_refs, out_refs, (held, total) = refs[: -2 - outs], refs[-2 - outs : -2], refs[-2:]
    tile = w_ref.shape[-1]
    block_tiles = x_refs[0].shape[0] // tile
    gather_blocks(x_refs, held)
    total[...] = jnp.zeros_like(total)
    spare = total.shape[0] // tile - 1

    def body(w, t, used, n):
        row = row_ref[t]
        if places[n] == 3:
            row = row % block_tiles
        row = jnp.where(used, row + n * 2 * block_tiles, spare)
        part = jnp.dot(w, held[aligned(col_ref[t], tile), :], preferred_element_type=F32)
        total[aligned(row, tile), :] += part

    finish(body)
    rows = block_tiles * tile
    for n, place in enumerate(places):
        first = n * 2 * rows
        for out_ref in out_refs:
            out_ref[n * rows : (n + 1) * rows, :] = total[first : first + rows, :].astype(BF)
            first += rows


def backward_kernel(places, unroll, bounds_ref, row_ref, col_ref, w_ref, *refs):
    refs, (total, held, tiles_held, sems) = refs[:-4], refs[-4:]
    ranges = [(bounds_ref[place], bounds_ref[4 + place]) for place in places]
    finish = stream_slots(w_ref, tiles_held, sems, ranges, unroll)
    tile = w_ref.shape[-1]
    block_refs, refs = refs[: 2 if places == (0,) else 3], refs[2 if places == (0,) else 3 :]
    if places == (0,):
        out_refs, token_ref = refs[:-1], refs[-1]
        token_ref[...] = jnp.zeros_like(token_ref)
        total[...] = jnp.zeros_like(total)
    else:
        old_refs, out_refs = refs[: len(refs) // 2], refs[len(refs) // 2 :]
        first = 0
        for old_ref in old_refs:
            total[first : first + old_ref.shape[0], :] = old_ref[...].astype(F32)
            first += old_ref.shape[0]
        total[first:, :] = jnp.zeros((total.shape[0] - first, total.shape[1]), F32)
    gather_blocks(block_refs, held)
    spare = total.shape[0] // tile - 1
    block_tiles = held.shape[0] // tile // (2 if places == (0,) else 5)

    def body(w, t, used, n):
        row = row_ref[t]
        if places[n] == 3:
            row = row % block_tiles + 4 * block_tiles
        elif places[n] > 0:
            row = jnp.where(row < block_tiles, row, row + block_tiles) + n * block_tiles
        part = lax.dot_general(
            w, held[aligned(row, tile), :], (((0,), (0,)), ((), ())), preferred_element_type=F32
        )
        total[aligned(jnp.where(used, col_ref[t], spare), tile), :] += part

    finish(body)
    first = 0
    for out_ref in out_refs:
        rows = out_ref.shape[0]
        out_ref[...] = total[first : first + rows, :].astype(out_ref.dtype)
        first += rows


def dense_kernel(*refs):
    part_refs, (norm_ref, weight_ref, bias_ref, up_ref) = refs[:-8], refs[-8:-4]
    hidden_ref, grad_ref, aggregated_ref, pre_grad_ref = refs[-4:]
    norm = norm_ref[...]
    neighbor = part_refs[0][...].astype(F32)
    for part_ref in part_refs[1:]:
        part = part_ref[...].astype(F32)
        neighbor = neighbor + part
    aggregated = (norm * neighbor).astype(BF)
    weight = weight_ref[...]
    pre_act = jnp.dot(aggregated, weight, preferred_element_type=F32) + bias_ref[...]
    gate = 0.5 * jnp.tanh(0.5 * pre_act) + 0.5
    hidden_ref[...] = (pre_act * gate).astype(BF)
    pre_grad = (up_ref[...].astype(F32) * (gate + pre_act * gate * (1.0 - gate))).astype(BF)
    back = lax.dot_general(pre_grad, weight, (((1,), (1,)), ((), ())), preferred_element_type=F32)
    grad_ref[...] = (norm * back).astype(BF)
    aggregated_ref[...] = aggregated
    pre_grad_ref[...] = pre_grad


def weight_kernel(core_ref, aggregated_ref, pre_grad_ref, keep_ref, send_ref, full):
    pre_grad = pre_grad_ref[...]
    half = full.shape[0] // CORES
    full[...] = lax.dot_general(
        aggregated_ref[...], pre_grad, (((0,), (0,)), ((), ())), preferred_element_type=F32
    )
    sums = jnp.sum(pre_grad.astype(F32), axis=0, keepdims=True)
    sums = jnp.broadcast_to(sums, (BIAS_ROWS, pre_grad.shape[1]))
    core = core_ref[0]
    for out_ref, side in ((keep_ref, core), (send_ref, 1 - core)):
        out_ref[:half, :] = full[aligned(side, half), :]
        out_ref[half:, :] = sums


def on_device(
    features, degrees, tile_weights, tile_rows, tile_cols, tile_counts, weight, layer_bias, upstream
):
    row_count, feat_width = features.shape
    hid_width = weight.shape[1]
    slot_total, tile = tile_weights.shape[2], tile_weights.shape[-1]
    row_tiles = row_count // tile
    rep_count, blk_count = lax.axis_size("rep"), lax.axis_size("blk")
    rep_index, blk_index = lax.axis_index("rep"), lax.axis_index("blk")
    core, pair_index = blk_index % CORES, blk_index // CORES
    col_tiles = rep_count * row_tiles
    block_shape = jax.ShapeDtypeStruct((row_count, feat_width), BF)

    rows_dev, cols_dev, count_dev = tile_rows[0, 0], tile_cols[0, 0], tile_counts[0, 0]
    used = jnp.arange(slot_total, dtype=jnp.int32) < count_dev
    group = rows_dev // row_tiles
    row_place = jnp.where(group % CORES == core, 0, row_tiles) + rows_dev % row_tiles
    col_place = rep_place(cols_dev // row_tiles, rep_index, core) * row_tiles + cols_dev % row_tiles
    pair_ids = jnp.stack([pair_at(place, pair_index, core) for place in range(4)])
    pair_ids = jnp.concatenate([pair_ids, pair_ids + 1])
    bounds = jnp.sum(used & (group // CORES < pair_ids[:, None]), axis=1).astype(jnp.int32)
    row_place, col_place = row_place.astype(jnp.int32), col_place.astype(jnp.int32)

    scaled, norm_wide = pl.pallas_call(
        prepare_kernel,
        out_shape=[block_shape, jax.ShapeDtypeStruct((row_count, feat_width), F32)],
        in_specs=[HBM] * 2,
        out_specs=[VMEM] * 2,
        scratch_shapes=[
            pltpu.VMEM((row_tiles, tile), jnp.int32),
            pltpu.VMEM((row_count, feat_width), BF),
            pltpu.SemaphoreType.DMA((2,)),
        ],
        compiler_params=params(16),
        cost_estimate=SMALL,
        name="prepare",
    )(in_hbm(degrees.reshape(row_tiles, tile)), in_hbm(features))

    source = {place: move(scaled, rep_partner(place)) for place in far_first(rep_count)}
    source = [scaled] + [source[place] for place in range(1, rep_count)]

    def stage(earlier):
        return pl.pallas_call(
            stage_kernel,
            out_shape=jax.ShapeDtypeStruct((slot_total, tile, tile), BF),
            in_specs=[HBM, ANY],
            out_specs=VMEM,
            scratch_shapes=[pltpu.SemaphoreType.DMA],
            compiler_params=params(16),
            cost_estimate=cost(0, 2 * slot_total * tile * tile * 2),
            name="stage_tiles",
        )(in_hbm(tile_weights[0, 0]), earlier)

    tiles_dev = stage(scaled)

    tiles_hbm = in_hbm(tile_weights[0, 0])

    def fetch_scratch(unroll, ranges):
        fetches = slot_total // unroll + ranges
        return [pltpu.VMEM((fetches, unroll, tile, tile), BF), pltpu.SemaphoreType.DMA((fetches,))]

    def forward(places, unroll, stream, earlier):
        outs = 1 if 3 in places else 2
        shape = jax.ShapeDtypeStruct((len(places) * row_count, feat_width), BF)
        return pl.pallas_call(
            functools.partial(forward_kernel, places, unroll, stream),
            out_shape=[shape] * outs,
            in_specs=[ANY, SMEM, SMEM, SMEM] + [HBM if stream else VMEM] + [VMEM] * rep_count,
            out_specs=[VMEM] * outs,
            scratch_shapes=[
                pltpu.VMEM((col_tiles * tile, feat_width), BF),
                pltpu.VMEM(((outs * len(places) * row_tiles + 1) * tile, feat_width), F32),
            ]
            + (fetch_scratch(unroll, len(places)) if stream else []),
            compiler_params=params(28 if stream else 16),
            cost_estimate=SMALL,
            name="forward_" + "_".join(map(str, places)),
        )(earlier, bounds, row_place, col_place, tiles_hbm if stream else tiles_dev, *source)

    def add(a, b):
        return (a.astype(F32) + b.astype(F32)).astype(BF)

    (part3,) = forward((3,), 12, False, norm_wide)
    came3 = move(part3, pair_partner(3, False))

    def pair_sums(keep, send):
        other = swap_cores(send)
        near, far = add(keep[:row_count], other[:row_count]), add(keep[row_count:], other[row_count:])
        return near, far, other[:TOKEN_ROWS]

    near, far, token = block(pair_sums, *forward((1, 2), 16, False, part3))
    came2 = move(far, pair_partner(2, False))
    came1 = move(near, pair_partner(1, False))

    def own_sum(earlier):
        keep, send = forward((0,), 20, True, earlier)
        return add(keep, swap_cores(send))

    own = block(own_sum, token)
    (came3,) = together([came3], [own])
    (came2,) = together([came2], [came3])
    (came1,) = together([came1], [came2])

    hidden, scaled_grad, aggregated, pre_grad = pl.pallas_call(
        dense_kernel,
        out_shape=[
            pltpu.VMEM((row_count, hid_width), BF),
            block_shape,
            block_shape,
            jax.ShapeDtypeStruct((row_count, hid_width), BF),
        ],
        in_specs=[VMEM] * 9,
        out_specs=[VMEM] * 4,
        compiler_params=params(16),
        cost_estimate=SMALL,
        name="dense",
    )(own, came1, came2, came3, scaled, norm_wide, weight, layer_bias[None], upstream)

    grads2 = move(scaled_grad, pair_partner(2, True))
    grads3 = move(scaled_grad, pair_partner(3, True))
    grads1 = move(scaled_grad, pair_partner(1, True))

    def backward(places, unroll, out_shape, *blocks):
        held_rows = (2 if places == (0,) else 5) * row_count
        return pl.pallas_call(
            functools.partial(backward_kernel, places, unroll),
            out_shape=out_shape,
            in_specs=[SMEM, SMEM, SMEM, HBM] + [VMEM] * len(blocks),
            out_specs=[VMEM] * len(out_shape),
            scratch_shapes=[
                pltpu.VMEM(((col_tiles + 1) * tile, feat_width), F32),
                pltpu.VMEM((held_rows, feat_width), BF),
            ]
            + fetch_scratch(unroll, len(places)),
            compiler_params=params(28),
            cost_estimate=SMALL,
            name="backward_" + "_".join(map(str, places)),
        )(bounds, row_place, col_place, tiles_hbm, *blocks)

    grad_rows = feat_width // CORES
    half_shape = jax.ShapeDtypeStruct((grad_rows + BIAS_ROWS, hid_width), F32)

    def own_pair(scaled_grad, aggregated, pre_grad):
        other = swap_cores(scaled_grad)
        keep, send = pl.pallas_call(
            weight_kernel,
            out_shape=[half_shape] * 2,
            in_specs=[SMEM, VMEM, VMEM],
            out_specs=[VMEM] * 2,
            scratch_shapes=[pltpu.VMEM((feat_width, hid_width), F32)],
            compiler_params=params(16),
            cost_estimate=SMALL,
            name="weight_terms",
        )(core[None].astype(jnp.int32), aggregated, pre_grad)
        grad = keep + swap_cores(send)
        token_shape = jax.ShapeDtypeStruct((TOKEN_ROWS, feat_width), BF)
        *total, token = backward((0,), 16, [block_shape] * rep_count + [token_shape], scaled_grad, other)
        for n in range(rep_bits()):
            came = move(grad.astype(BF), rep_partner(1 << n))
            if n == 0:
                (grad,) = together([grad], [token])
            grad = grad + came.astype(F32)
        return total, grad

    total, grad = block(own_pair, scaled_grad, aggregated, pre_grad)
    blk_bits = (blk_count - 1).bit_length()
    grads1, grads2, grads3 = together([grads1, grads2, grads3], [grad])
    near_far = jnp.concatenate([grads1, grads2])
    came = move(grad.astype(BF), lambda r, k: (r, k ^ 2))
    column_shapes = [jax.ShapeDtypeStruct((row_count, feat_width), F32)] + [block_shape] * (rep_count - 1)
    columns = backward((1, 2, 3), 16, column_shapes, near_far, swap_cores(near_far), grads3, *total)
    columns = together(columns, [came])

    def write(value):
        return pl.pallas_call(
            write_kernel,
            out_shape=jax.ShapeDtypeStruct(value.shape, value.dtype),
            in_specs=[VMEM],
            out_specs=HBM,
            scratch_shapes=[pltpu.SemaphoreType.DMA],
            compiler_params=params(16),
            cost_estimate=SMALL,
            name="write_hidden",
        )(value)

    def finish(grad, came, hidden):
        grad = grad + came.astype(F32)
        for bit in range(2, blk_bits):
            grad = grad + move(grad.astype(BF), lambda r, k: (r, k ^ (1 << bit))).astype(F32)
        grad = grad * (row_count * rep_count * blk_count) ** (-0.5)
        mine = grad[:grad_rows]
        other = swap_cores(mine)
        weight_grad = jnp.where(
            core == 0, jnp.concatenate([mine, other]), jnp.concatenate([other, mine])
        )
        return weight_grad, grad[grad_rows], write(hidden)

    column_sum = columns[0]
    arrived = {place: move(columns[place], rep_partner(place)) for place in far_first(rep_count)}
    weight_grad, bias_grad, hidden = block(finish, grad, came, hidden)
    for place in range(1, rep_count):
        column_sum = column_sum + arrived[place].astype(F32)
    feature_grad = (norm_wide * (column_sum + scaled_grad.astype(F32))).astype(BF)
    return (hidden, feature_grad, weight_grad, bias_grad)


def solution(mesh):
    placed = (
        P(("rep", "blk"), None),
        P(("rep", "blk")),
        P("rep", "blk", None, None, None),
        P("rep", "blk", None),
        P("rep", "blk", None),
        P("rep", "blk"),
        P(),
        P(),
        P(("rep", "blk"), None),
    )
    return jax.shard_map(
        on_device,
        mesh=mesh,
        in_specs=placed,
        out_specs=(P(("rep", "blk"), None), P(("rep", "blk"), None), P(), P()),
        check_vma=False,
    )
```

```python
import functools

import jax
import jax.numpy as jnp
from jax import lax
from jax.experimental import pallas as pl
from jax.experimental.pallas import tpu as pltpu
from jax.sharding import PartitionSpec as P

BOTH = ("rep", "blk")
VMEM = pl.BlockSpec(memory_space=pltpu.VMEM)
SMEM = pl.BlockSpec(memory_space=pltpu.SMEM)
ANY = pl.BlockSpec(memory_space=pl.ANY)
HBM = pl.BlockSpec(memory_space=pltpu.HBM)
BF = jnp.bfloat16
F32 = jnp.float32
CORES = 2
BIAS_ROWS = 16
TOKEN_ROWS = 16


def params(mib):
    return pltpu.CompilerParams(vmem_limit_bytes=mib * 1024 * 1024)


def cost(flops, size):
    return pl.CostEstimate(flops=flops, bytes_accessed=size, transcendentals=0)


SMALL = cost(0, 1024)
LARGE = cost(0, 2**26)


def node_scale(degrees):
    return 1.0 / jnp.sqrt(degrees.astype(F32) + 1.0)


def in_hbm(value):
    return pltpu.with_memory_space_constraint(value, pltpu.HBM)


def move(value, target):
    rep_count, blk_count = lax.axis_size("rep"), lax.axis_size("blk")
    pairs = []
    for r in range(rep_count):
        for k in range(blk_count):
            to_r, to_k = target(r, k)
            pairs.append((r * blk_count + k, to_r * blk_count + to_k))
    return lax.ppermute(value, BOTH, pairs)


def block(function, *args):
    shapes = jax.eval_shape(function, *args)
    return lax.cond(
        lax.axis_index("blk") < lax.axis_size("blk"),
        function,
        lambda *unused: jax.tree.map(lambda shape: jnp.zeros(shape.shape, shape.dtype), shapes),
        *args,
    )


def swap_cores(value):
    return move(value, lambda r, k: (r, k ^ 1))


def rep_bits():
    return (lax.axis_size("rep") - 1).bit_length()


def rep_partner(place):
    bits = rep_bits()
    turned = sum(((place >> n) & 1) << ((n + 1) % bits) for n in range(bits))
    return lambda r, k: (r ^ (turned if k % 2 else place), k)


def rep_place(rep_ids, rep_index, core):
    bits = rep_bits()
    relative = rep_ids ^ rep_index
    place = jnp.zeros_like(relative)
    for n in range(bits):
        turned = (relative >> ((n + 1) % bits)) & 1
        place = place + (jnp.where(core == 0, (relative >> n) & 1, turned) << n)
    return place


def far_first(count):
    return sorted(range(1, count), key=lambda place: -bin(place).count("1"))


def pair_at(place, pair_index, core):
    pairs = lax.axis_size("blk") // CORES
    if pairs == 4:
        return pair_index ^ (0, 1, 3, 2)[place]
    step = (0, 1, -1, jnp.where(core == 0, -2, 2))[place]
    return (pair_index + step) % pairs


def pair_partner(place, back, other_core=False):
    blk_count = lax.axis_size("blk")
    if other_core:
        near = pair_partner(place, back)
        return lambda r, k: (r, near(r, k)[1] ^ 1)

    def target(r, k):
        if place == 3:
            return (r, (k + (3 if k % 2 else -3)) % blk_count)
        if blk_count == 8:
            return (r, k ^ {1: 2, 2: 6}[place])
        step = {1: 2, 2: -2}[place]
        return (r, (k + (-step if back else step)) % blk_count)

    return target


def together(values, earlier=(), weigh=None):
    count = len(values)
    return pl.pallas_call(
        lambda *refs: None,
        out_shape=[jax.ShapeDtypeStruct(value.shape, value.dtype) for value in values],
        in_specs=[ANY] * (count + len(earlier)),
        out_specs=[ANY] * count,
        input_output_aliases={n: n for n in range(count)},
        compiler_params=params(16),
        cost_estimate=weigh or SMALL,
        name="together",
    )(*values, *earlier)


def prepare_kernel(degrees_hbm, features_hbm, scaled_ref, norm_ref, degrees_ref, features_ref, sems):
    copies = [
        pltpu.make_async_copy(degrees_hbm, degrees_ref, sems.at[0]),
        pltpu.make_async_copy(features_hbm, features_ref, sems.at[1]),
    ]
    for copy in copies:
        copy.start()
    for copy in copies:
        copy.wait()
    tile = degrees_ref.shape[1]
    for n in range(degrees_ref.shape[0]):
        norm = node_scale(degrees_ref[n : n + 1, :])
        norm = jnp.broadcast_to(norm, (tile, tile)).T
        rows = slice(n * tile, (n + 1) * tile)
        norm_ref[rows, :] = norm
        scaled_ref[rows, :] = (norm * features_ref[rows, :].astype(F32)).astype(BF)


def write_kernel(value_ref, out_ref, sem):
    copy = pltpu.make_async_copy(value_ref, out_ref, sem)
    copy.start()
    copy.wait()


def scalars_kernel(*refs):
    refs, sems = refs[:-1], refs[-1]
    count = len(refs) // 2
    copies = [pltpu.make_async_copy(refs[n], refs[count + n], sems.at[n]) for n in range(count)]
    for copy in copies:
        copy.start()
    for copy in copies:
        copy.wait()


def stage_kernel(w_ref, earlier_ref, out_ref, sem):
    copy = pltpu.make_async_copy(w_ref, out_ref, sem)
    copy.start()
    copy.wait()


def gather_blocks(block_refs, held):
    first = 0
    for block_ref in block_refs:
        held[first : first + block_ref.shape[0], :] = block_ref[...]
        first += block_ref.shape[0]


def aligned(index, tile):
    return pl.ds(pl.multiple_of(index * tile, tile), tile)


def stream_slots(w_hbm, held, sems, ranges, unroll):
    slot_total = w_hbm.shape[0]
    begins = [0]
    for low, high in ranges:
        begins.append(begins[-1] + (high - low + unroll - 1) // unroll)

    def fetch(low, i, place):
        first = jnp.minimum(low + i * unroll, slot_total - unroll)
        return first, pltpu.make_async_copy(w_hbm.at[pl.ds(first, unroll)], held.at[place], sems.at[place])

    for n, (low, high) in enumerate(ranges):

        def start(i, carry, low=low, begin=begins[n]):
            fetch(low, i, begin + i)[1].start()
            return carry

        lax.fori_loop(0, begins[n + 1] - begins[n], start, 0)

    def finish(body):
        for n, (low, high) in enumerate(ranges):

            def step(i, carry, low=low, high=high, n=n, begin=begins[n]):
                first, copy = fetch(low, i, begin + i)
                copy.wait()
                for u in range(unroll):
                    t = first + u
                    body(held[begin + i, u], t, (t >= low + i * unroll) & (t < high), n)
                return carry

            lax.fori_loop(0, begins[n + 1] - begins[n], step, 0)

    return finish


def held_slots(w_ref, ranges, unroll):
    slot_total = w_ref.shape[0]

    def finish(body):
        for n, (low, high) in enumerate(ranges):

            def step(i, carry, low=low, high=high, n=n):
                for u in range(unroll):
                    t = low + i * unroll + u
                    place = jnp.minimum(t, slot_total - 1)
                    body(w_ref[place], place, t < high, n)
                return carry

            lax.fori_loop(0, (high - low + unroll - 1) // unroll, step, 0)

    return finish


def forward_kernel(places, unroll, stream, earlier_ref, bounds_ref, row_ref, col_ref, w_ref, *refs):
    ranges = [(bounds_ref[place], bounds_ref[4 + place]) for place in places]
    if stream:
        refs, (tiles_held, sems) = refs[:-2], refs[-2:]
        finish = stream_slots(w_ref, tiles_held, sems, ranges, unroll)
    else:
        finish = held_slots(w_ref, ranges, unroll)
    outs = 1 if 3 in places else 2
    x_refs, out_refs, (held, total) = refs[: -2 - outs], refs[-2 - outs : -2], refs[-2:]
    tile = w_ref.shape[-1]
    block_tiles = x_refs[0].shape[0] // tile
    gather_blocks(x_refs, held)
    total[...] = jnp.zeros_like(total)
    spare = total.shape[0] // tile - 1

    def body(w, t, used, n):
        row = row_ref[t]
        if places[n] == 3:
            row = row % block_tiles
        row = jnp.where(used, row + n * 2 * block_tiles, spare)
        part = jnp.dot(w, held[aligned(col_ref[t], tile), :], preferred_element_type=F32)
        total[aligned(row, tile), :] += part

    finish(body)
    rows = block_tiles * tile
    for n, place in enumerate(places):
        first = n * 2 * rows
        for out_ref in out_refs:
            out_ref[n * rows : (n + 1) * rows, :] = total[first : first + rows, :].astype(BF)
            first += rows


def backward_kernel(places, unroll, bounds_ref, row_ref, col_ref, w_ref, *refs):
    refs, (total, held, tiles_held, sems) = refs[:-4], refs[-4:]
    ranges = [(bounds_ref[place], bounds_ref[4 + place]) for place in places]
    finish = stream_slots(w_ref, tiles_held, sems, ranges, unroll)
    tile = w_ref.shape[-1]
    block_refs, refs = refs[: 2 if places == (0,) else 3], refs[2 if places == (0,) else 3 :]
    if places == (0,):
        out_refs, token_ref = refs[:-1], refs[-1]
        token_ref[...] = jnp.zeros_like(token_ref)
        total[...] = jnp.zeros_like(total)
    else:
        old_refs, out_refs = refs[: len(refs) // 2], refs[len(refs) // 2 :]
        first = 0
        for old_ref in old_refs:
            total[first : first + old_ref.shape[0], :] = old_ref[...].astype(F32)
            first += old_ref.shape[0]
        total[first:, :] = jnp.zeros((total.shape[0] - first, total.shape[1]), F32)
    gather_blocks(block_refs, held)
    spare = total.shape[0] // tile - 1
    block_tiles = held.shape[0] // tile // (2 if places == (0,) else 5)

    def body(w, t, used, n):
        row = row_ref[t]
        if places[n] == 3:
            row = row % block_tiles + 4 * block_tiles
        elif places[n] > 0:
            row = jnp.where(row < block_tiles, row, row + block_tiles) + n * block_tiles
        part = lax.dot_general(
            w, held[aligned(row, tile), :], (((0,), (0,)), ((), ())), preferred_element_type=F32
        )
        total[aligned(jnp.where(used, col_ref[t], spare), tile), :] += part

    finish(body)
    first = 0
    for out_ref in out_refs:
        rows = out_ref.shape[0]
        out_ref[...] = total[first : first + rows, :].astype(out_ref.dtype)
        first += rows


def dense_kernel(*refs):
    part_refs, (norm_ref, weight_ref, bias_ref, up_ref) = refs[:-8], refs[-8:-4]
    hidden_ref, grad_ref, aggregated_ref, pre_grad_ref = refs[-4:]
    norm = norm_ref[...]
    neighbor = part_refs[0][...].astype(F32)
    for part_ref in part_refs[1:]:
        part = part_ref[...].astype(F32)
        neighbor = neighbor + part
    aggregated = (norm * neighbor).astype(BF)
    weight = weight_ref[...]
    pre_act = jnp.dot(aggregated, weight, preferred_element_type=F32) + bias_ref[...]
    gate = 0.5 * jnp.tanh(0.5 * pre_act) + 0.5
    hidden_ref[...] = (pre_act * gate).astype(BF)
    pre_grad = (up_ref[...].astype(F32) * (gate + pre_act * gate * (1.0 - gate))).astype(BF)
    back = lax.dot_general(pre_grad, weight, (((1,), (1,)), ((), ())), preferred_element_type=F32)
    grad_ref[...] = (norm * back).astype(BF)
    aggregated_ref[...] = aggregated
    pre_grad_ref[...] = pre_grad


def weight_kernel(core_ref, aggregated_ref, pre_grad_ref, keep_ref, send_ref, full):
    pre_grad = pre_grad_ref[...]
    half = full.shape[0] // CORES
    full[...] = lax.dot_general(
        aggregated_ref[...], pre_grad, (((0,), (0,)), ((), ())), preferred_element_type=F32
    )
    sums = jnp.sum(pre_grad.astype(F32), axis=0, keepdims=True)
    sums = jnp.broadcast_to(sums, (BIAS_ROWS, pre_grad.shape[1]))
    core = core_ref[0]
    for out_ref, side in ((keep_ref, core), (send_ref, 1 - core)):
        out_ref[:half, :] = full[aligned(side, half), :]
        out_ref[half:, :] = sums


def on_device(
    features, degrees, tile_weights, tile_rows, tile_cols, tile_counts, weight, layer_bias, upstream
):
    row_count, feat_width = features.shape
    hid_width = weight.shape[1]
    slot_total, tile = tile_weights.shape[2], tile_weights.shape[-1]
    row_tiles = row_count // tile
    rep_count, blk_count = lax.axis_size("rep"), lax.axis_size("blk")
    rep_index, blk_index = lax.axis_index("rep"), lax.axis_index("blk")
    core, pair_index = blk_index % CORES, blk_index // CORES
    col_tiles = rep_count * row_tiles
    block_shape = jax.ShapeDtypeStruct((row_count, feat_width), BF)

    rows_dev, cols_dev, count_dev = tile_rows[0, 0], tile_cols[0, 0], tile_counts[0, 0]
    used = jnp.arange(slot_total, dtype=jnp.int32) < count_dev
    group = rows_dev // row_tiles
    row_place = jnp.where(group % CORES == core, 0, row_tiles) + rows_dev % row_tiles
    col_place = rep_place(cols_dev // row_tiles, rep_index, core) * row_tiles + cols_dev % row_tiles
    pair_ids = jnp.stack([pair_at(place, pair_index, core) for place in range(4)])
    pair_ids = jnp.concatenate([pair_ids, pair_ids + 1])
    bounds = jnp.sum(used & (group // CORES < pair_ids[:, None]), axis=1).astype(jnp.int32)
    row_place, col_place = row_place.astype(jnp.int32), col_place.astype(jnp.int32)
    bounds, row_place, col_place = pl.pallas_call(
        scalars_kernel,
        out_shape=[pltpu.SMEM(value.shape, jnp.int32) for value in (bounds, row_place, col_place)],
        in_specs=[ANY] * 3,
        out_specs=[SMEM] * 3,
        scratch_shapes=[pltpu.SemaphoreType.DMA((3,))],
        compiler_params=params(16),
        cost_estimate=SMALL,
        name="scalars",
    )(bounds, row_place, col_place)

    scaled, norm_wide = pl.pallas_call(
        prepare_kernel,
        out_shape=[block_shape, jax.ShapeDtypeStruct((row_count, feat_width), F32)],
        in_specs=[HBM] * 2,
        out_specs=[VMEM] * 2,
        scratch_shapes=[
            pltpu.VMEM((row_tiles, tile), jnp.int32),
            pltpu.VMEM((row_count, feat_width), BF),
            pltpu.SemaphoreType.DMA((2,)),
        ],
        compiler_params=params(16),
        cost_estimate=SMALL,
        name="prepare",
    )(in_hbm(degrees.reshape(row_tiles, tile)), in_hbm(features))

    source = {place: move(scaled, rep_partner(place)) for place in far_first(rep_count)}
    source = [scaled] + [source[place] for place in range(1, rep_count)]

    def stage(earlier):
        return pl.pallas_call(
            stage_kernel,
            out_shape=jax.ShapeDtypeStruct((slot_total, tile, tile), BF),
            in_specs=[HBM, ANY],
            out_specs=VMEM,
            scratch_shapes=[pltpu.SemaphoreType.DMA],
            compiler_params=params(16),
            cost_estimate=cost(0, 2 * slot_total * tile * tile * 2),
            name="stage_tiles",
        )(in_hbm(tile_weights[0, 0]), earlier)

    tiles_dev = stage(scaled)

    tiles_hbm = in_hbm(tile_weights[0, 0])

    def fetch_scratch(unroll, ranges):
        fetches = slot_total // unroll + ranges
        return [pltpu.VMEM((fetches, unroll, tile, tile), BF), pltpu.SemaphoreType.DMA((fetches,))]

    def forward(places, unroll, stream, earlier):
        outs = 1 if 3 in places else 2
        shape = jax.ShapeDtypeStruct((len(places) * row_count, feat_width), BF)
        return pl.pallas_call(
            functools.partial(forward_kernel, places, unroll, stream),
            out_shape=[shape] * outs,
            in_specs=[ANY, SMEM, SMEM, SMEM] + [HBM if stream else VMEM] + [VMEM] * rep_count,
            out_specs=[VMEM] * outs,
            scratch_shapes=[
                pltpu.VMEM((col_tiles * tile, feat_width), BF),
                pltpu.VMEM(((outs * len(places) * row_tiles + 1) * tile, feat_width), F32),
            ]
            + (fetch_scratch(unroll, len(places)) if stream else []),
            compiler_params=params(28 if stream else 16),
            cost_estimate=SMALL,
            name="forward_" + "_".join(map(str, places)),
        )(earlier, bounds, row_place, col_place, tiles_hbm if stream else tiles_dev, *source)

    def add(a, b):
        return (a.astype(F32) + b.astype(F32)).astype(BF)

    (part3,) = forward((3,), 12, False, norm_wide)
    came3 = move(part3, pair_partner(3, False))

    def pair_sums(keep, send):
        other = swap_cores(send)
        near, far = add(keep[:row_count], other[:row_count]), add(keep[row_count:], other[row_count:])
        return near, far, other[:TOKEN_ROWS]

    near, far, token = block(pair_sums, *forward((1, 2), 16, False, part3))
    came2 = move(far, pair_partner(2, False))
    came1 = move(near, pair_partner(1, False))

    def own_sum(earlier):
        keep, send = forward((0,), 20, True, earlier)
        return add(keep, swap_cores(send))

    own = block(own_sum, token)
    (came3,) = together([came3], [own])
    (came2,) = together([came2], [came3])
    (came1,) = together([came1], [came2])

    hidden, scaled_grad, aggregated, pre_grad = pl.pallas_call(
        dense_kernel,
        out_shape=[
            pltpu.VMEM((row_count, hid_width), BF),
            block_shape,
            block_shape,
            jax.ShapeDtypeStruct((row_count, hid_width), BF),
        ],
        in_specs=[VMEM] * 9,
        out_specs=[VMEM] * 4,
        compiler_params=params(16),
        cost_estimate=SMALL,
        name="dense",
    )(own, came1, came2, came3, scaled, norm_wide, weight, layer_bias[None], upstream)

    grads2 = move(scaled_grad, pair_partner(2, True))
    grads3 = move(scaled_grad, pair_partner(3, True))
    grads1 = move(scaled_grad, pair_partner(1, True))

    def backward(places, unroll, out_shape, *blocks):
        held_rows = (2 if places == (0,) else 5) * row_count
        return pl.pallas_call(
            functools.partial(backward_kernel, places, unroll),
            out_shape=out_shape,
            in_specs=[SMEM, SMEM, SMEM, HBM] + [VMEM] * len(blocks),
            out_specs=[VMEM] * len(out_shape),
            scratch_shapes=[
                pltpu.VMEM(((col_tiles + 1) * tile, feat_width), F32),
                pltpu.VMEM((held_rows, feat_width), BF),
            ]
            + fetch_scratch(unroll, len(places)),
            compiler_params=params(28),
            cost_estimate=SMALL,
            name="backward_" + "_".join(map(str, places)),
        )(bounds, row_place, col_place, tiles_hbm, *blocks)

    grad_rows = feat_width // CORES
    half_shape = jax.ShapeDtypeStruct((grad_rows + BIAS_ROWS, hid_width), F32)

    def own_pair(scaled_grad, aggregated, pre_grad):
        other = swap_cores(scaled_grad)
        keep, send = pl.pallas_call(
            weight_kernel,
            out_shape=[half_shape] * 2,
            in_specs=[SMEM, VMEM, VMEM],
            out_specs=[VMEM] * 2,
            scratch_shapes=[pltpu.VMEM((feat_width, hid_width), F32)],
            compiler_params=params(16),
            cost_estimate=SMALL,
            name="weight_terms",
        )(core[None].astype(jnp.int32), aggregated, pre_grad)
        grad = keep + swap_cores(send)
        token_shape = jax.ShapeDtypeStruct((TOKEN_ROWS, feat_width), BF)
        *total, token = backward((0,), 16, [block_shape] * rep_count + [token_shape], scaled_grad, other)
        for n in range(rep_bits()):
            came = move(grad.astype(BF), rep_partner(1 << n))
            if n == 0:
                (grad,) = together([grad], [token])
            grad = grad + came.astype(F32)
        return total, grad

    total, grad = block(own_pair, scaled_grad, aggregated, pre_grad)
    blk_bits = (blk_count - 1).bit_length()
    grads1, grads2, grads3 = together([grads1, grads2, grads3], [grad])
    near_far = jnp.concatenate([grads1, grads2])
    came = move(grad.astype(BF), lambda r, k: (r, k ^ 2))
    column_shapes = [jax.ShapeDtypeStruct((row_count, feat_width), F32)] + [block_shape] * (rep_count - 1)
    columns = backward((1, 2, 3), 16, column_shapes, near_far, swap_cores(near_far), grads3, *total)
    columns = together(columns, [came])

    def write(value):
        return pl.pallas_call(
            write_kernel,
            out_shape=jax.ShapeDtypeStruct(value.shape, value.dtype),
            in_specs=[VMEM],
            out_specs=HBM,
            scratch_shapes=[pltpu.SemaphoreType.DMA],
            compiler_params=params(16),
            cost_estimate=SMALL,
            name="write_hidden",
        )(value)

    def finish(grad, came, hidden):
        grad = grad + came.astype(F32)
        for bit in range(2, blk_bits):
            grad = grad + move(grad.astype(BF), lambda r, k: (r, k ^ (1 << bit))).astype(F32)
        grad = grad * (row_count * rep_count * blk_count) ** (-0.5)
        mine = grad[:grad_rows]
        other = swap_cores(mine)
        weight_grad = jnp.where(
            core == 0, jnp.concatenate([mine, other]), jnp.concatenate([other, mine])
        )
        return weight_grad, grad[grad_rows], write(hidden)

    column_sum = columns[0]
    arrived = {place: move(columns[place], rep_partner(place)) for place in far_first(rep_count)}
    weight_grad, bias_grad, hidden = block(finish, grad, came, hidden)
    for place in range(1, rep_count):
        column_sum = column_sum + arrived[place].astype(F32)
    feature_grad = (norm_wide * (column_sum + scaled_grad.astype(F32))).astype(BF)
    return (hidden, feature_grad, weight_grad, bias_grad)


def solution(mesh):
    placed = (
        P(("rep", "blk"), None),
        P(("rep", "blk")),
        P("rep", "blk", None, None, None),
        P("rep", "blk", None),
        P("rep", "blk", None),
        P("rep", "blk"),
        P(),
        P(),
        P(("rep", "blk"), None),
    )
    return jax.shard_map(
        on_device,
        mesh=mesh,
        in_specs=placed,
        out_specs=(P(("rep", "blk"), None), P(("rep", "blk"), None), P(), P()),
        check_vma=False,
    )
```

```python
import functools

import jax
import jax.numpy as jnp
from jax import lax
from jax.experimental import pallas as pl
from jax.experimental.pallas import tpu as pltpu
from jax.sharding import PartitionSpec as P

BOTH = ("rep", "blk")
VMEM = pl.BlockSpec(memory_space=pltpu.VMEM)
SMEM = pl.BlockSpec(memory_space=pltpu.SMEM)
ANY = pl.BlockSpec(memory_space=pl.ANY)
HBM = pl.BlockSpec(memory_space=pltpu.HBM)
BF = jnp.bfloat16
F32 = jnp.float32
CORES = 2
BIAS_ROWS = 16
TOKEN_ROWS = 16


def params(mib):
    return pltpu.CompilerParams(vmem_limit_bytes=mib * 1024 * 1024)


def cost(flops, size):
    return pl.CostEstimate(flops=flops, bytes_accessed=size, transcendentals=0)


SMALL = cost(0, 1024)
LARGE = cost(0, 2**26)


def node_scale(degrees):
    return 1.0 / jnp.sqrt(degrees.astype(F32) + 1.0)


def in_hbm(value):
    return pltpu.with_memory_space_constraint(value, pltpu.HBM)


def move(value, target):
    rep_count, blk_count = lax.axis_size("rep"), lax.axis_size("blk")
    pairs = []
    for r in range(rep_count):
        for k in range(blk_count):
            to_r, to_k = target(r, k)
            pairs.append((r * blk_count + k, to_r * blk_count + to_k))
    return lax.ppermute(value, BOTH, pairs)


def block(function, *args):
    shapes = jax.eval_shape(function, *args)
    return lax.cond(
        lax.axis_index("blk") < lax.axis_size("blk"),
        function,
        lambda *unused: jax.tree.map(lambda shape: jnp.zeros(shape.shape, shape.dtype), shapes),
        *args,
    )


def swap_cores(value):
    return move(value, lambda r, k: (r, k ^ 1))


def rep_bits():
    return (lax.axis_size("rep") - 1).bit_length()


def rep_partner(place):
    bits = rep_bits()
    turned = sum(((place >> n) & 1) << ((n + 1) % bits) for n in range(bits))
    return lambda r, k: (r ^ (turned if k % 2 else place), k)


def rep_place(rep_ids, rep_index, core):
    bits = rep_bits()
    relative = rep_ids ^ rep_index
    place = jnp.zeros_like(relative)
    for n in range(bits):
        turned = (relative >> ((n + 1) % bits)) & 1
        place = place + (jnp.where(core == 0, (relative >> n) & 1, turned) << n)
    return place


def far_first(count):
    return sorted(range(1, count), key=lambda place: -bin(place).count("1"))


def pair_at(place, pair_index, core):
    pairs = lax.axis_size("blk") // CORES
    if pairs == 4:
        return pair_index ^ (0, 1, 3, 2)[place]
    step = (0, 1, -1, jnp.where(core == 0, -2, 2))[place]
    return (pair_index + step) % pairs


def pair_partner(place, back, other_core=False):
    blk_count = lax.axis_size("blk")
    if other_core:
        near = pair_partner(place, back)
        return lambda r, k: (r, near(r, k)[1] ^ 1)

    def target(r, k):
        if place == 3:
            return (r, (k + (3 if k % 2 else -3)) % blk_count)
        if blk_count == 8:
            return (r, k ^ {1: 2, 2: 6}[place])
        step = {1: 2, 2: -2}[place]
        return (r, (k + (-step if back else step)) % blk_count)

    return target


def together(values, earlier=(), weigh=None):
    count = len(values)
    return pl.pallas_call(
        lambda *refs: None,
        out_shape=[jax.ShapeDtypeStruct(value.shape, value.dtype) for value in values],
        in_specs=[ANY] * (count + len(earlier)),
        out_specs=[ANY] * count,
        input_output_aliases={n: n for n in range(count)},
        compiler_params=params(16),
        cost_estimate=weigh or SMALL,
        name="together",
    )(*values, *earlier)


def prepare_kernel(degrees_hbm, features_hbm, scaled_ref, norm_ref, degrees_ref, features_ref, sems):
    copies = [
        pltpu.make_async_copy(degrees_hbm, degrees_ref, sems.at[0]),
        pltpu.make_async_copy(features_hbm, features_ref, sems.at[1]),
    ]
    for copy in copies:
        copy.start()
    tile = degrees_ref.shape[1]
    copies[0].wait()
    for n in range(degrees_ref.shape[0]):
        norm = jnp.broadcast_to(node_scale(degrees_ref[n : n + 1, :]), (tile, tile)).T
        norm_ref[n * tile : (n + 1) * tile, :] = norm
    copies[1].wait()
    scaled_ref[...] = (norm_ref[...] * features_ref[...].astype(F32)).astype(BF)


def write_kernel(value_ref, out_ref, sem):
    copy = pltpu.make_async_copy(value_ref, out_ref, sem)
    copy.start()
    copy.wait()


def scalars_kernel(*refs):
    refs, sems = refs[:-1], refs[-1]
    count = len(refs) // 2
    copies = [pltpu.make_async_copy(refs[n], refs[count + n], sems.at[n]) for n in range(count)]
    for copy in copies:
        copy.start()
    for copy in copies:
        copy.wait()


def stage_kernel(w_ref, earlier_ref, out_ref, sem):
    copy = pltpu.make_async_copy(w_ref, out_ref, sem)
    copy.start()
    copy.wait()


def gather_blocks(block_refs, held):
    first = 0
    for block_ref in block_refs:
        held[first : first + block_ref.shape[0], :] = block_ref[...]
        first += block_ref.shape[0]


def aligned(index, tile):
    return pl.ds(pl.multiple_of(index * tile, tile), tile)


def stream_slots(w_hbm, held, sems, ranges, unroll):
    slot_total = w_hbm.shape[0]
    begins = [0]
    for low, high in ranges:
        begins.append(begins[-1] + (high - low + unroll - 1) // unroll)

    def fetch(low, i, place):
        first = jnp.minimum(low + i * unroll, slot_total - unroll)
        return first, pltpu.make_async_copy(w_hbm.at[pl.ds(first, unroll)], held.at[place], sems.at[place])

    for n, (low, high) in enumerate(ranges):

        def start(i, carry, low=low, begin=begins[n]):
            fetch(low, i, begin + i)[1].start()
            return carry

        lax.fori_loop(0, begins[n + 1] - begins[n], start, 0)

    def finish(body):
        for n, (low, high) in enumerate(ranges):

            def step(i, carry, low=low, high=high, n=n, begin=begins[n]):
                first, copy = fetch(low, i, begin + i)
                copy.wait()
                for u in range(unroll):
                    t = first + u
                    body(held[begin + i, u], t, (t >= low + i * unroll) & (t < high), n)
                return carry

            lax.fori_loop(0, begins[n + 1] - begins[n], step, 0)

    return finish


def held_slots(w_ref, ranges, unroll):
    slot_total = w_ref.shape[0]

    def finish(body):
        for n, (low, high) in enumerate(ranges):

            def step(i, carry, low=low, high=high, n=n):
                for u in range(unroll):
                    t = low + i * unroll + u
                    place = jnp.minimum(t, slot_total - 1)
                    body(w_ref[place], place, t < high, n)
                return carry

            lax.fori_loop(0, (high - low + unroll - 1) // unroll, step, 0)

    return finish


def forward_kernel(places, unroll, stream, earlier_ref, bounds_ref, row_ref, col_ref, w_ref, *refs):
    ranges = [(bounds_ref[place], bounds_ref[4 + place]) for place in places]
    if stream:
        refs, (tiles_held, sems) = refs[:-2], refs[-2:]
        finish = stream_slots(w_ref, tiles_held, sems, ranges, unroll)
    else:
        finish = held_slots(w_ref, ranges, unroll)
    outs = 1 if 3 in places else 2
    x_refs, out_refs, (held, total) = refs[: -2 - outs], refs[-2 - outs : -2], refs[-2:]
    tile = w_ref.shape[-1]
    block_tiles = x_refs[0].shape[0] // tile
    gather_blocks(x_refs, held)
    total[...] = jnp.zeros_like(total)
    spare = total.shape[0] // tile - 1

    def body(w, t, used, n):
        row = row_ref[t]
        if places[n] == 3:
            row = row % block_tiles
        row = jnp.where(used, row + n * 2 * block_tiles, spare)
        part = jnp.dot(w, held[aligned(col_ref[t], tile), :], preferred_element_type=F32)
        total[aligned(row, tile), :] += part

    finish(body)
    rows = block_tiles * tile
    for n, place in enumerate(places):
        first = n * 2 * rows
        for out_ref in out_refs:
            out_ref[n * rows : (n + 1) * rows, :] = total[first : first + rows, :].astype(BF)
            first += rows


def backward_kernel(places, unroll, bounds_ref, row_ref, col_ref, w_ref, *refs):
    refs, (total, held, tiles_held, sems) = refs[:-4], refs[-4:]
    ranges = [(bounds_ref[place], bounds_ref[4 + place]) for place in places]
    finish = stream_slots(w_ref, tiles_held, sems, ranges, unroll)
    tile = w_ref.shape[-1]
    block_refs, refs = refs[: 2 if places == (0,) else 3], refs[2 if places == (0,) else 3 :]
    if places == (0,):
        out_refs, token_ref = refs[:-1], refs[-1]
        token_ref[...] = jnp.zeros_like(token_ref)
        total[...] = jnp.zeros_like(total)
    else:
        old_refs, out_refs = refs[: len(refs) // 2], refs[len(refs) // 2 :]
        first = 0
        for old_ref in old_refs:
            total[first : first + old_ref.shape[0], :] = old_ref[...].astype(F32)
            first += old_ref.shape[0]
        total[first:, :] = jnp.zeros((total.shape[0] - first, total.shape[1]), F32)
    gather_blocks(block_refs, held)
    spare = total.shape[0] // tile - 1
    block_tiles = held.shape[0] // tile // (2 if places == (0,) else 5)

    def body(w, t, used, n):
        row = row_ref[t]
        if places[n] == 3:
            row = row % block_tiles + 4 * block_tiles
        elif places[n] > 0:
            row = jnp.where(row < block_tiles, row, row + block_tiles) + n * block_tiles
        part = lax.dot_general(
            w, held[aligned(row, tile), :], (((0,), (0,)), ((), ())), preferred_element_type=F32
        )
        total[aligned(jnp.where(used, col_ref[t], spare), tile), :] += part

    finish(body)
    first = 0
    for out_ref in out_refs:
        rows = out_ref.shape[0]
        out_ref[...] = total[first : first + rows, :].astype(out_ref.dtype)
        first += rows


def dense_kernel(*refs):
    part_refs, (norm_ref, weight_ref, bias_ref, up_ref) = refs[:-8], refs[-8:-4]
    hidden_ref, grad_ref, aggregated_ref, pre_grad_ref = refs[-4:]
    norm = norm_ref[...]
    neighbor = part_refs[0][...].astype(F32)
    for part_ref in part_refs[1:]:
        part = part_ref[...].astype(F32)
        neighbor = neighbor + part
    aggregated = (norm * neighbor).astype(BF)
    weight = weight_ref[...]
    pre_act = jnp.dot(aggregated, weight, preferred_element_type=F32) + bias_ref[...]
    gate = 0.5 * jnp.tanh(0.5 * pre_act) + 0.5
    hidden_ref[...] = (pre_act * gate).astype(BF)
    pre_grad = (up_ref[...].astype(F32) * (gate + pre_act * gate * (1.0 - gate))).astype(BF)
    back = lax.dot_general(pre_grad, weight, (((1,), (1,)), ((), ())), preferred_element_type=F32)
    grad_ref[...] = (norm * back).astype(BF)
    aggregated_ref[...] = aggregated
    pre_grad_ref[...] = pre_grad


def weight_kernel(core_ref, aggregated_ref, pre_grad_ref, keep_ref, send_ref, full):
    pre_grad = pre_grad_ref[...]
    half = full.shape[0] // CORES
    full[...] = lax.dot_general(
        aggregated_ref[...], pre_grad, (((0,), (0,)), ((), ())), preferred_element_type=F32
    )
    sums = jnp.sum(pre_grad.astype(F32), axis=0, keepdims=True)
    sums = jnp.broadcast_to(sums, (BIAS_ROWS, pre_grad.shape[1]))
    core = core_ref[0]
    for out_ref, side in ((keep_ref, core), (send_ref, 1 - core)):
        out_ref[:half, :] = full[aligned(side, half), :]
        out_ref[half:, :] = sums


def on_device(
    features, degrees, tile_weights, tile_rows, tile_cols, tile_counts, weight, layer_bias, upstream
):
    row_count, feat_width = features.shape
    hid_width = weight.shape[1]
    slot_total, tile = tile_weights.shape[2], tile_weights.shape[-1]
    row_tiles = row_count // tile
    rep_count, blk_count = lax.axis_size("rep"), lax.axis_size("blk")
    rep_index, blk_index = lax.axis_index("rep"), lax.axis_index("blk")
    core, pair_index = blk_index % CORES, blk_index // CORES
    col_tiles = rep_count * row_tiles
    block_shape = jax.ShapeDtypeStruct((row_count, feat_width), BF)

    rows_dev, cols_dev, count_dev = tile_rows[0, 0], tile_cols[0, 0], tile_counts[0, 0]
    used = jnp.arange(slot_total, dtype=jnp.int32) < count_dev
    group = rows_dev // row_tiles
    row_place = jnp.where(group % CORES == core, 0, row_tiles) + rows_dev % row_tiles
    col_place = rep_place(cols_dev // row_tiles, rep_index, core) * row_tiles + cols_dev % row_tiles
    pair_ids = jnp.stack([pair_at(place, pair_index, core) for place in range(4)])
    pair_ids = jnp.concatenate([pair_ids, pair_ids + 1])
    bounds = jnp.sum(used & (group // CORES < pair_ids[:, None]), axis=1).astype(jnp.int32)
    row_place, col_place = row_place.astype(jnp.int32), col_place.astype(jnp.int32)
    bounds, row_place, col_place = pl.pallas_call(
        scalars_kernel,
        out_shape=[pltpu.SMEM(value.shape, jnp.int32) for value in (bounds, row_place, col_place)],
        in_specs=[ANY] * 3,
        out_specs=[SMEM] * 3,
        scratch_shapes=[pltpu.SemaphoreType.DMA((3,))],
        compiler_params=params(16),
        cost_estimate=SMALL,
        name="scalars",
    )(bounds, row_place, col_place)

    scaled, norm_wide = pl.pallas_call(
        prepare_kernel,
        out_shape=[block_shape, jax.ShapeDtypeStruct((row_count, feat_width), F32)],
        in_specs=[HBM] * 2,
        out_specs=[VMEM] * 2,
        scratch_shapes=[
            pltpu.VMEM((row_tiles, tile), jnp.int32),
            pltpu.VMEM((row_count, feat_width), BF),
            pltpu.SemaphoreType.DMA((2,)),
        ],
        compiler_params=params(16),
        cost_estimate=SMALL,
        name="prepare",
    )(in_hbm(degrees.reshape(row_tiles, tile)), in_hbm(features))

    source = {place: move(scaled, rep_partner(place)) for place in far_first(rep_count)}
    source = [scaled] + [source[place] for place in range(1, rep_count)]

    def stage(earlier):
        return pl.pallas_call(
            stage_kernel,
            out_shape=jax.ShapeDtypeStruct((slot_total, tile, tile), BF),
            in_specs=[HBM, ANY],
            out_specs=VMEM,
            scratch_shapes=[pltpu.SemaphoreType.DMA],
            compiler_params=params(16),
            cost_estimate=cost(0, 2 * slot_total * tile * tile * 2),
            name="stage_tiles",
        )(in_hbm(tile_weights[0, 0]), earlier)

    tiles_dev = stage(scaled)

    tiles_hbm = in_hbm(tile_weights[0, 0])

    def fetch_scratch(unroll, ranges):
        fetches = slot_total // unroll + ranges
        return [pltpu.VMEM((fetches, unroll, tile, tile), BF), pltpu.SemaphoreType.DMA((fetches,))]

    def forward(places, unroll, stream, earlier):
        outs = 1 if 3 in places else 2
        shape = jax.ShapeDtypeStruct((len(places) * row_count, feat_width), BF)
        return pl.pallas_call(
            functools.partial(forward_kernel, places, unroll, stream),
            out_shape=[shape] * outs,
            in_specs=[ANY, SMEM, SMEM, SMEM] + [HBM if stream else VMEM] + [VMEM] * rep_count,
            out_specs=[VMEM] * outs,
            scratch_shapes=[
                pltpu.VMEM((col_tiles * tile, feat_width), BF),
                pltpu.VMEM(((outs * len(places) * row_tiles + 1) * tile, feat_width), F32),
            ]
            + (fetch_scratch(unroll, len(places)) if stream else []),
            compiler_params=params(28 if stream else 16),
            cost_estimate=SMALL,
            name="forward_" + "_".join(map(str, places)),
        )(earlier, bounds, row_place, col_place, tiles_hbm if stream else tiles_dev, *source)

    def add(a, b):
        return (a.astype(F32) + b.astype(F32)).astype(BF)

    (part3,) = forward((3,), 12, False, norm_wide)
    came3 = move(part3, pair_partner(3, False))

    def pair_sums(keep, send):
        other = swap_cores(send)
        near, far = add(keep[:row_count], other[:row_count]), add(keep[row_count:], other[row_count:])
        return near, far, other[:TOKEN_ROWS]

    near, far, token = block(pair_sums, *forward((1, 2), 16, False, part3))
    came2 = move(far, pair_partner(2, False))
    came1 = move(near, pair_partner(1, False))

    def own_sum(earlier):
        keep, send = forward((0,), 20, True, earlier)
        return add(keep, swap_cores(send))

    own = block(own_sum, token)
    (came3,) = together([came3], [own])
    (came2,) = together([came2], [came3])
    (came1,) = together([came1], [came2])

    hidden, scaled_grad, aggregated, pre_grad = pl.pallas_call(
        dense_kernel,
        out_shape=[
            pltpu.VMEM((row_count, hid_width), BF),
            block_shape,
            block_shape,
            jax.ShapeDtypeStruct((row_count, hid_width), BF),
        ],
        in_specs=[VMEM] * 9,
        out_specs=[VMEM] * 4,
        compiler_params=params(16),
        cost_estimate=SMALL,
        name="dense",
    )(own, came1, came2, came3, scaled, norm_wide, weight, layer_bias[None], upstream)

    grads2 = move(scaled_grad, pair_partner(2, True))
    grads3 = move(scaled_grad, pair_partner(3, True))
    grads1 = move(scaled_grad, pair_partner(1, True))

    def backward(places, unroll, out_shape, *blocks):
        held_rows = (2 if places == (0,) else 5) * row_count
        return pl.pallas_call(
            functools.partial(backward_kernel, places, unroll),
            out_shape=out_shape,
            in_specs=[SMEM, SMEM, SMEM, HBM] + [VMEM] * len(blocks),
            out_specs=[VMEM] * len(out_shape),
            scratch_shapes=[
                pltpu.VMEM(((col_tiles + 1) * tile, feat_width), F32),
                pltpu.VMEM((held_rows, feat_width), BF),
            ]
            + fetch_scratch(unroll, len(places)),
            compiler_params=params(28),
            cost_estimate=SMALL,
            name="backward_" + "_".join(map(str, places)),
        )(bounds, row_place, col_place, tiles_hbm, *blocks)

    grad_rows = feat_width // CORES
    half_shape = jax.ShapeDtypeStruct((grad_rows + BIAS_ROWS, hid_width), F32)

    def own_pair(scaled_grad, aggregated, pre_grad):
        other = swap_cores(scaled_grad)
        keep, send = pl.pallas_call(
            weight_kernel,
            out_shape=[half_shape] * 2,
            in_specs=[SMEM, VMEM, VMEM],
            out_specs=[VMEM] * 2,
            scratch_shapes=[pltpu.VMEM((feat_width, hid_width), F32)],
            compiler_params=params(16),
            cost_estimate=SMALL,
            name="weight_terms",
        )(core[None].astype(jnp.int32), aggregated, pre_grad)
        grad = keep + swap_cores(send)
        token_shape = jax.ShapeDtypeStruct((TOKEN_ROWS, feat_width), BF)
        *total, token = backward((0,), 16, [block_shape] * rep_count + [token_shape], scaled_grad, other)
        for n in range(rep_bits()):
            came = move(grad.astype(BF), rep_partner(1 << n))
            if n == 0:
                (grad,) = together([grad], [token])
            grad = grad + came.astype(F32)
        return total, grad

    total, grad = block(own_pair, scaled_grad, aggregated, pre_grad)
    blk_bits = (blk_count - 1).bit_length()
    grads1, grads2, grads3 = together([grads1, grads2, grads3], [grad])
    near_far = jnp.concatenate([grads1, grads2])
    came = move(grad.astype(BF), lambda r, k: (r, k ^ 2))
    column_shapes = [jax.ShapeDtypeStruct((row_count, feat_width), F32)] + [block_shape] * (rep_count - 1)
    columns = backward((1, 2, 3), 16, column_shapes, near_far, swap_cores(near_far), grads3, *total)
    columns = together(columns, [came])

    def write(value):
        return pl.pallas_call(
            write_kernel,
            out_shape=jax.ShapeDtypeStruct(value.shape, value.dtype),
            in_specs=[VMEM],
            out_specs=HBM,
            scratch_shapes=[pltpu.SemaphoreType.DMA],
            compiler_params=params(16),
            cost_estimate=SMALL,
            name="write_hidden",
        )(value)

    def finish(grad, came, hidden):
        grad = grad + came.astype(F32)
        for bit in range(2, blk_bits):
            grad = grad + move(grad.astype(BF), lambda r, k: (r, k ^ (1 << bit))).astype(F32)
        grad = grad * (row_count * rep_count * blk_count) ** (-0.5)
        mine = grad[:grad_rows]
        other = swap_cores(mine)
        weight_grad = jnp.where(
            core == 0, jnp.concatenate([mine, other]), jnp.concatenate([other, mine])
        )
        return weight_grad, grad[grad_rows], write(hidden)

    column_sum = columns[0]
    arrived = {place: move(columns[place], rep_partner(place)) for place in far_first(rep_count)}
    weight_grad, bias_grad, hidden = block(finish, grad, came, hidden)
    for place in range(1, rep_count):
        column_sum = column_sum + arrived[place].astype(F32)
    feature_grad = (norm_wide * (column_sum + scaled_grad.astype(F32))).astype(BF)
    return (hidden, feature_grad, weight_grad, bias_grad)


def solution(mesh):
    placed = (
        P(("rep", "blk"), None),
        P(("rep", "blk")),
        P("rep", "blk", None, None, None),
        P("rep", "blk", None),
        P("rep", "blk", None),
        P("rep", "blk"),
        P(),
        P(),
        P(("rep", "blk"), None),
    )
    return jax.shard_map(
        on_device,
        mesh=mesh,
        in_specs=placed,
        out_specs=(P(("rep", "blk"), None), P(("rep", "blk"), None), P(), P()),
        check_vma=False,
    )
```

```python
import functools

import jax
import jax.numpy as jnp
from jax import lax
from jax.experimental import pallas as pl
from jax.experimental.pallas import tpu as pltpu
from jax.sharding import PartitionSpec as P

BOTH = ("rep", "blk")
VMEM = pl.BlockSpec(memory_space=pltpu.VMEM)
SMEM = pl.BlockSpec(memory_space=pltpu.SMEM)
ANY = pl.BlockSpec(memory_space=pl.ANY)
HBM = pl.BlockSpec(memory_space=pltpu.HBM)
BF = jnp.bfloat16
F32 = jnp.float32
CORES = 2
BIAS_ROWS = 16
TOKEN_ROWS = 16


def params(mib):
    return pltpu.CompilerParams(vmem_limit_bytes=mib * 1024 * 1024)


def cost(flops, size):
    return pl.CostEstimate(flops=flops, bytes_accessed=size, transcendentals=0)


SMALL = cost(0, 1024)
LARGE = cost(0, 2**26)


def node_scale(degrees):
    return 1.0 / jnp.sqrt(degrees.astype(F32) + 1.0)


def in_hbm(value):
    return pltpu.with_memory_space_constraint(value, pltpu.HBM)


def move(value, target):
    rep_count, blk_count = lax.axis_size("rep"), lax.axis_size("blk")
    pairs = []
    for r in range(rep_count):
        for k in range(blk_count):
            to_r, to_k = target(r, k)
            pairs.append((r * blk_count + k, to_r * blk_count + to_k))
    return lax.ppermute(value, BOTH, pairs)


def block(function, *args):
    shapes = jax.eval_shape(function, *args)
    return lax.cond(
        lax.axis_index("blk") < lax.axis_size("blk"),
        function,
        lambda *unused: jax.tree.map(lambda shape: jnp.zeros(shape.shape, shape.dtype), shapes),
        *args,
    )


def swap_cores(value):
    return move(value, lambda r, k: (r, k ^ 1))


def rep_bits():
    return (lax.axis_size("rep") - 1).bit_length()


def rep_partner(place):
    bits = rep_bits()
    turned = sum(((place >> n) & 1) << ((n + 1) % bits) for n in range(bits))
    return lambda r, k: (r ^ (turned if k % 2 else place), k)


def rep_place(rep_ids, rep_index, core):
    bits = rep_bits()
    relative = rep_ids ^ rep_index
    place = jnp.zeros_like(relative)
    for n in range(bits):
        turned = (relative >> ((n + 1) % bits)) & 1
        place = place + (jnp.where(core == 0, (relative >> n) & 1, turned) << n)
    return place


def far_first(count):
    return sorted(range(1, count), key=lambda place: -bin(place).count("1"))


def pair_at(place, pair_index, core):
    pairs = lax.axis_size("blk") // CORES
    if pairs == 4:
        return pair_index ^ (0, 1, 3, 2)[place]
    step = (0, 1, -1, jnp.where(core == 0, -2, 2))[place]
    return (pair_index + step) % pairs


def pair_partner(place, back, other_core=False):
    blk_count = lax.axis_size("blk")
    if other_core:
        near = pair_partner(place, back)
        return lambda r, k: (r, near(r, k)[1] ^ 1)

    def target(r, k):
        if place == 3:
            return (r, (k + (3 if k % 2 else -3)) % blk_count)
        if blk_count == 8:
            return (r, k ^ {1: 2, 2: 6}[place])
        step = {1: 2, 2: -2}[place]
        return (r, (k + (-step if back else step)) % blk_count)

    return target


def together(values, earlier=(), weigh=None):
    count = len(values)
    return pl.pallas_call(
        lambda *refs: None,
        out_shape=[jax.ShapeDtypeStruct(value.shape, value.dtype) for value in values],
        in_specs=[ANY] * (count + len(earlier)),
        out_specs=[ANY] * count,
        input_output_aliases={n: n for n in range(count)},
        compiler_params=params(16),
        cost_estimate=weigh or SMALL,
        name="together",
    )(*values, *earlier)


def prepare_kernel(degrees_hbm, features_hbm, scaled_ref, norm_ref, degrees_ref, features_ref, sems):
    copies = [
        pltpu.make_async_copy(degrees_hbm, degrees_ref, sems.at[0]),
        pltpu.make_async_copy(features_hbm, features_ref, sems.at[1]),
    ]
    for copy in copies:
        copy.start()
    tile = degrees_ref.shape[1]
    copies[0].wait()
    for n in range(degrees_ref.shape[0]):
        norm = jnp.broadcast_to(node_scale(degrees_ref[n : n + 1, :]), (tile, tile)).T
        norm_ref[n * tile : (n + 1) * tile, :] = norm
    copies[1].wait()
    scaled_ref[...] = (norm_ref[...] * features_ref[...].astype(F32)).astype(BF)


def write_kernel(value_ref, out_ref, sem):
    copy = pltpu.make_async_copy(value_ref, out_ref, sem)
    copy.start()
    copy.wait()


def scalars_kernel(*refs):
    refs, sems = refs[:-1], refs[-1]
    count = len(refs) // 2
    copies = [pltpu.make_async_copy(refs[n], refs[count + n], sems.at[n]) for n in range(count)]
    for copy in copies:
        copy.start()
    for copy in copies:
        copy.wait()


def stage_kernel(w_ref, earlier_ref, out_ref, sem):
    copy = pltpu.make_async_copy(w_ref, out_ref, sem)
    copy.start()
    copy.wait()


def gather_blocks(block_refs, held):
    first = 0
    for block_ref in block_refs:
        held[first : first + block_ref.shape[0], :] = block_ref[...]
        first += block_ref.shape[0]


def aligned(index, tile):
    return pl.ds(pl.multiple_of(index * tile, tile), tile)


def stream_slots(w_hbm, held, sems, ranges, unroll):
    slot_total = w_hbm.shape[0]
    begins = [0]
    for low, high in ranges:
        begins.append(begins[-1] + (high - low + unroll - 1) // unroll)

    def fetch(low, i, place):
        first = jnp.minimum(low + i * unroll, slot_total - unroll)
        return first, pltpu.make_async_copy(w_hbm.at[pl.ds(first, unroll)], held.at[place], sems.at[place])

    for n, (low, high) in enumerate(ranges):

        def start(i, carry, low=low, begin=begins[n]):
            fetch(low, i, begin + i)[1].start()
            return carry

        lax.fori_loop(0, begins[n + 1] - begins[n], start, 0)

    def finish(body):
        for n, (low, high) in enumerate(ranges):

            def step(i, carry, low=low, high=high, n=n, begin=begins[n]):
                first, copy = fetch(low, i, begin + i)
                copy.wait()
                for u in range(unroll):
                    t = first + u
                    body(held[begin + i, u], t, (t >= low + i * unroll) & (t < high), n)
                return carry

            lax.fori_loop(0, begins[n + 1] - begins[n], step, 0)

    return finish


def held_slots(w_ref, ranges, unroll):
    slot_total = w_ref.shape[0]

    def finish(body):
        for n, (low, high) in enumerate(ranges):

            def step(i, carry, low=low, high=high, n=n):
                for u in range(unroll):
                    t = low + i * unroll + u
                    place = jnp.minimum(t, slot_total - 1)
                    body(w_ref[place], place, t < high, n)
                return carry

            lax.fori_loop(0, (high - low + unroll - 1) // unroll, step, 0)

    return finish


def forward_kernel(places, unroll, stream, earlier_ref, bounds_ref, row_ref, col_ref, w_ref, *refs):
    ranges = [(bounds_ref[place], bounds_ref[4 + place]) for place in places]
    if stream:
        refs, (tiles_held, sems) = refs[:-2], refs[-2:]
        finish = stream_slots(w_ref, tiles_held, sems, ranges, unroll)
    else:
        finish = held_slots(w_ref, ranges, unroll)
    outs = 1 if 3 in places else 2
    x_refs, out_refs, (held, total) = refs[: -2 - outs], refs[-2 - outs : -2], refs[-2:]
    tile = w_ref.shape[-1]
    block_tiles = x_refs[0].shape[0] // tile
    gather_blocks(x_refs, held)
    total[...] = jnp.zeros_like(total)
    spare = total.shape[0] // tile - 1

    def body(w, t, used, n):
        row = row_ref[t]
        if places[n] == 3:
            row = row % block_tiles
        row = jnp.where(used, row + n * 2 * block_tiles, spare)
        part = jnp.dot(w, held[aligned(col_ref[t], tile), :], preferred_element_type=F32)
        total[aligned(row, tile), :] += part

    finish(body)
    rows = block_tiles * tile
    for n, place in enumerate(places):
        first = n * 2 * rows
        for out_ref in out_refs:
            out_ref[n * rows : (n + 1) * rows, :] = total[first : first + rows, :].astype(BF)
            first += rows


def backward_kernel(places, unroll, bounds_ref, row_ref, col_ref, w_ref, *refs):
    refs, (total, held, tiles_held, sems) = refs[:-4], refs[-4:]
    ranges = [(bounds_ref[place], bounds_ref[4 + place]) for place in places]
    finish = stream_slots(w_ref, tiles_held, sems, ranges, unroll)
    tile = w_ref.shape[-1]
    block_refs, refs = refs[: 2 if places == (0,) else 3], refs[2 if places == (0,) else 3 :]
    if places == (0,):
        out_refs, token_ref = refs[:-1], refs[-1]
        token_ref[...] = jnp.zeros_like(token_ref)
        total[...] = jnp.zeros_like(total)
    else:
        old_refs, out_refs = refs[: len(refs) // 2], refs[len(refs) // 2 :]
        first = 0
        for old_ref in old_refs:
            total[first : first + old_ref.shape[0], :] = old_ref[...].astype(F32)
            first += old_ref.shape[0]
        total[first:, :] = jnp.zeros((total.shape[0] - first, total.shape[1]), F32)
    gather_blocks(block_refs, held)
    spare = total.shape[0] // tile - 1
    block_tiles = held.shape[0] // tile // (2 if places == (0,) else 5)

    def body(w, t, used, n):
        row = row_ref[t]
        if places[n] == 3:
            row = row % block_tiles + 4 * block_tiles
        elif places[n] > 0:
            row = jnp.where(row < block_tiles, row, row + block_tiles) + n * block_tiles
        part = lax.dot_general(
            w, held[aligned(row, tile), :], (((0,), (0,)), ((), ())), preferred_element_type=F32
        )
        total[aligned(jnp.where(used, col_ref[t], spare), tile), :] += part

    finish(body)
    first = 0
    for out_ref in out_refs:
        rows = out_ref.shape[0]
        out_ref[...] = total[first : first + rows, :].astype(out_ref.dtype)
        first += rows


def dense_kernel(*refs):
    part_refs, (norm_ref, weight_ref, bias_ref, up_ref) = refs[:-8], refs[-8:-4]
    hidden_ref, grad_ref, aggregated_ref, pre_grad_ref = refs[-4:]
    norm = norm_ref[...]
    neighbor = part_refs[0][...].astype(F32)
    for part_ref in part_refs[1:]:
        part = part_ref[...].astype(F32)
        neighbor = neighbor + part
    aggregated = (norm * neighbor).astype(BF)
    weight = weight_ref[...]
    pre_act = jnp.dot(aggregated, weight, preferred_element_type=F32) + bias_ref[...]
    gate = 0.5 * jnp.tanh(0.5 * pre_act) + 0.5
    hidden_ref[...] = (pre_act * gate).astype(BF)
    pre_grad = (up_ref[...].astype(F32) * (gate + pre_act * gate * (1.0 - gate))).astype(BF)
    back = lax.dot_general(pre_grad, weight, (((1,), (1,)), ((), ())), preferred_element_type=F32)
    grad_ref[...] = (norm * back).astype(BF)
    aggregated_ref[...] = aggregated
    pre_grad_ref[...] = pre_grad


def weight_kernel(core_ref, aggregated_ref, pre_grad_ref, keep_ref, send_ref, full):
    pre_grad = pre_grad_ref[...]
    half = full.shape[0] // CORES
    full[...] = lax.dot_general(
        aggregated_ref[...], pre_grad, (((0,), (0,)), ((), ())), preferred_element_type=F32
    )
    sums = jnp.sum(pre_grad.astype(F32), axis=0, keepdims=True)
    sums = jnp.broadcast_to(sums, (BIAS_ROWS, pre_grad.shape[1]))
    core = core_ref[0]
    for out_ref, side in ((keep_ref, core), (send_ref, 1 - core)):
        out_ref[:half, :] = full[aligned(side, half), :]
        out_ref[half:, :] = sums


def on_device(
    features, degrees, tile_weights, tile_rows, tile_cols, tile_counts, weight, layer_bias, upstream
):
    row_count, feat_width = features.shape
    hid_width = weight.shape[1]
    slot_total, tile = tile_weights.shape[2], tile_weights.shape[-1]
    row_tiles = row_count // tile
    rep_count, blk_count = lax.axis_size("rep"), lax.axis_size("blk")
    rep_index, blk_index = lax.axis_index("rep"), lax.axis_index("blk")
    core, pair_index = blk_index % CORES, blk_index // CORES
    col_tiles = rep_count * row_tiles
    block_shape = jax.ShapeDtypeStruct((row_count, feat_width), BF)

    rows_dev, cols_dev, count_dev = tile_rows[0, 0], tile_cols[0, 0], tile_counts[0, 0]
    used = jnp.arange(slot_total, dtype=jnp.int32) < count_dev
    group = rows_dev // row_tiles
    row_place = jnp.where(group % CORES == core, 0, row_tiles) + rows_dev % row_tiles
    col_place = rep_place(cols_dev // row_tiles, rep_index, core) * row_tiles + cols_dev % row_tiles
    pair_ids = jnp.stack([pair_at(place, pair_index, core) for place in range(4)])
    pair_ids = jnp.concatenate([pair_ids, pair_ids + 1])
    bounds = jnp.sum(used & (group // CORES < pair_ids[:, None]), axis=1).astype(jnp.int32)
    row_place, col_place = row_place.astype(jnp.int32), col_place.astype(jnp.int32)
    bounds, row_place, col_place = pl.pallas_call(
        scalars_kernel,
        out_shape=[pltpu.SMEM(value.shape, jnp.int32) for value in (bounds, row_place, col_place)],
        in_specs=[ANY] * 3,
        out_specs=[SMEM] * 3,
        scratch_shapes=[pltpu.SemaphoreType.DMA((3,))],
        compiler_params=params(16),
        cost_estimate=SMALL,
        name="scalars",
    )(bounds, row_place, col_place)

    scaled, norm_wide = pl.pallas_call(
        prepare_kernel,
        out_shape=[block_shape, jax.ShapeDtypeStruct((row_count, feat_width), F32)],
        in_specs=[HBM] * 2,
        out_specs=[VMEM] * 2,
        scratch_shapes=[
            pltpu.VMEM((row_tiles, tile), jnp.int32),
            pltpu.VMEM((row_count, feat_width), BF),
            pltpu.SemaphoreType.DMA((2,)),
        ],
        compiler_params=params(16),
        cost_estimate=SMALL,
        name="prepare",
    )(in_hbm(degrees.reshape(row_tiles, tile)), in_hbm(features))

    source = {place: move(scaled, rep_partner(place)) for place in far_first(rep_count)}
    source = [scaled] + [source[place] for place in range(1, rep_count)]

    def stage(earlier):
        return pl.pallas_call(
            stage_kernel,
            out_shape=jax.ShapeDtypeStruct((slot_total, tile, tile), BF),
            in_specs=[HBM, ANY],
            out_specs=VMEM,
            scratch_shapes=[pltpu.SemaphoreType.DMA],
            compiler_params=params(16),
            cost_estimate=cost(0, 2 * slot_total * tile * tile * 2),
            name="stage_tiles",
        )(in_hbm(tile_weights[0, 0]), earlier)

    tiles_dev = stage(scaled)

    tiles_hbm = in_hbm(tile_weights[0, 0])

    def fetch_scratch(unroll, ranges):
        fetches = slot_total // unroll + ranges
        return [pltpu.VMEM((fetches, unroll, tile, tile), BF), pltpu.SemaphoreType.DMA((fetches,))]

    def forward(places, unroll, stream, earlier):
        outs = 1 if 3 in places else 2
        shape = jax.ShapeDtypeStruct((len(places) * row_count, feat_width), BF)
        return pl.pallas_call(
            functools.partial(forward_kernel, places, unroll, stream),
            out_shape=[shape] * outs,
            in_specs=[ANY, SMEM, SMEM, SMEM] + [HBM if stream else VMEM] + [VMEM] * rep_count,
            out_specs=[VMEM] * outs,
            scratch_shapes=[
                pltpu.VMEM((col_tiles * tile, feat_width), BF),
                pltpu.VMEM(((outs * len(places) * row_tiles + 1) * tile, feat_width), F32),
            ]
            + (fetch_scratch(unroll, len(places)) if stream else []),
            compiler_params=params(28 if stream else 16),
            cost_estimate=SMALL,
            name="forward_" + "_".join(map(str, places)),
        )(earlier, bounds, row_place, col_place, tiles_hbm if stream else tiles_dev, *source)

    def add(a, b):
        return (a.astype(F32) + b.astype(F32)).astype(BF)

    (part3,) = forward((3,), 12, False, norm_wide)
    came3 = move(part3, pair_partner(3, False))

    def pair_sums(keep, send):
        other = swap_cores(send)
        near, far = add(keep[:row_count], other[:row_count]), add(keep[row_count:], other[row_count:])
        return near, far, other[:TOKEN_ROWS]

    near, far, token = block(pair_sums, *forward((1, 2), 26, False, part3))
    came2 = move(far, pair_partner(2, False))
    came1 = move(near, pair_partner(1, False))

    def own_sum(earlier):
        keep, send = forward((0,), 20, True, earlier)
        return add(keep, swap_cores(send))

    own = block(own_sum, token)
    (came3,) = together([came3], [own])
    (came2,) = together([came2], [came3])
    (came1,) = together([came1], [came2])

    hidden, scaled_grad, aggregated, pre_grad = pl.pallas_call(
        dense_kernel,
        out_shape=[
            pltpu.VMEM((row_count, hid_width), BF),
            block_shape,
            block_shape,
            jax.ShapeDtypeStruct((row_count, hid_width), BF),
        ],
        in_specs=[VMEM] * 9,
        out_specs=[VMEM] * 4,
        compiler_params=params(16),
        cost_estimate=SMALL,
        name="dense",
    )(own, came1, came2, came3, scaled, norm_wide, weight, layer_bias[None], upstream)

    grads2 = move(scaled_grad, pair_partner(2, True))
    grads3 = move(scaled_grad, pair_partner(3, True))
    grads1 = move(scaled_grad, pair_partner(1, True))

    def backward(places, unroll, out_shape, *blocks):
        held_rows = (2 if places == (0,) else 5) * row_count
        return pl.pallas_call(
            functools.partial(backward_kernel, places, unroll),
            out_shape=out_shape,
            in_specs=[SMEM, SMEM, SMEM, HBM] + [VMEM] * len(blocks),
            out_specs=[VMEM] * len(out_shape),
            scratch_shapes=[
                pltpu.VMEM(((col_tiles + 1) * tile, feat_width), F32),
                pltpu.VMEM((held_rows, feat_width), BF),
            ]
            + fetch_scratch(unroll, len(places)),
            compiler_params=params(28),
            cost_estimate=SMALL,
            name="backward_" + "_".join(map(str, places)),
        )(bounds, row_place, col_place, tiles_hbm, *blocks)

    grad_rows = feat_width // CORES
    half_shape = jax.ShapeDtypeStruct((grad_rows + BIAS_ROWS, hid_width), F32)

    def own_pair(scaled_grad, aggregated, pre_grad):
        other = swap_cores(scaled_grad)
        keep, send = pl.pallas_call(
            weight_kernel,
            out_shape=[half_shape] * 2,
            in_specs=[SMEM, VMEM, VMEM],
            out_specs=[VMEM] * 2,
            scratch_shapes=[pltpu.VMEM((feat_width, hid_width), F32)],
            compiler_params=params(16),
            cost_estimate=SMALL,
            name="weight_terms",
        )(core[None].astype(jnp.int32), aggregated, pre_grad)
        grad = keep + swap_cores(send)
        token_shape = jax.ShapeDtypeStruct((TOKEN_ROWS, feat_width), BF)
        *total, token = backward((0,), 24, [block_shape] * rep_count + [token_shape], scaled_grad, other)
        for n in range(rep_bits()):
            came = move(grad.astype(BF), rep_partner(1 << n))
            if n == 0:
                (grad,) = together([grad], [token])
            grad = grad + came.astype(F32)
        return total, grad

    total, grad = block(own_pair, scaled_grad, aggregated, pre_grad)
    blk_bits = (blk_count - 1).bit_length()
    grads1, grads2, grads3 = together([grads1, grads2, grads3], [grad])
    near_far = jnp.concatenate([grads1, grads2])
    came = move(grad.astype(BF), lambda r, k: (r, k ^ 2))
    column_shapes = [jax.ShapeDtypeStruct((row_count, feat_width), F32)] + [block_shape] * (rep_count - 1)
    columns = backward((1, 2, 3), 16, column_shapes, near_far, swap_cores(near_far), grads3, *total)
    columns = together(columns, [came])

    def write(value):
        return pl.pallas_call(
            write_kernel,
            out_shape=jax.ShapeDtypeStruct(value.shape, value.dtype),
            in_specs=[VMEM],
            out_specs=HBM,
            scratch_shapes=[pltpu.SemaphoreType.DMA],
            compiler_params=params(16),
            cost_estimate=SMALL,
            name="write_hidden",
        )(value)

    def finish(grad, came, hidden):
        grad = grad + came.astype(F32)
        for bit in range(2, blk_bits):
            grad = grad + move(grad.astype(BF), lambda r, k: (r, k ^ (1 << bit))).astype(F32)
        grad = grad * (row_count * rep_count * blk_count) ** (-0.5)
        mine = grad[:grad_rows]
        other = swap_cores(mine)
        weight_grad = jnp.where(
            core == 0, jnp.concatenate([mine, other]), jnp.concatenate([other, mine])
        )
        return weight_grad, grad[grad_rows], write(hidden)

    column_sum = columns[0]
    arrived = {place: move(columns[place], rep_partner(place)) for place in far_first(rep_count)}
    weight_grad, bias_grad, hidden = block(finish, grad, came, hidden)
    for place in range(1, rep_count):
        column_sum = column_sum + arrived[place].astype(F32)
    feature_grad = (norm_wide * (column_sum + scaled_grad.astype(F32))).astype(BF)
    return (hidden, feature_grad, weight_grad, bias_grad)


def solution(mesh):
    placed = (
        P(("rep", "blk"), None),
        P(("rep", "blk")),
        P("rep", "blk", None, None, None),
        P("rep", "blk", None),
        P("rep", "blk", None),
        P("rep", "blk"),
        P(),
        P(),
        P(("rep", "blk"), None),
    )
    return jax.shard_map(
        on_device,
        mesh=mesh,
        in_specs=placed,
        out_specs=(P(("rep", "blk"), None), P(("rep", "blk"), None), P(), P()),
        check_vma=False,
    )
```
